32 devices in a mesh: board: 2 (over y), sub: 16 (over z, x, core).
Axes of the slice: x: 2, y: 2, z: 4, core: 2. Of those that a mesh axis runs over, the one named last changes fastest.
Arguments:
- rhs: float32 [2, 32, 4096], P('board', None, 'sub')
- schur: float32 [2, 12288, 768], P('board', 'sub'), as said below
- block_list: int32 [2, 96], P('board', 'sub'), may hold values from 0 to 31, as said below
- pad_rows: int32 [2, 1024], P('board', 'sub'), may hold values from 0 to 255, as said below
- pad_cond: float32 [2, 1024], P('board', 'sub'), may hold values from 0.5 to 2
- sink: float32 [2, 4096], P('board', 'sub'), may hold values from 0.2 to 2
- precond: float32 [2, 4096], P('board', 'sub'), may hold values from 0.3 to 1
Outputs:
- solution: float32 [2, 32, 4096], P('board', None, 'sub')
- residual: float32 [2, 32, 4096], P('board', None, 'sub')
The draws below stay inside these ranges and needn't reach their ends.
Inputs may be any that keep to these rules, and one draw needn't show every extreme that they name: `block_list`: every entry of a subdomain s's list is a block owned by a subdomain at most 3 away from s on the same board; the entries of one list are different and rising, and include all blocks that s owns. `pad_rows`: A subdomain's pad rows are different and rising, and include its first and last owned row. `schur`: each Schur block is symmetric and positive definite.
All inputs are finite; a program needn't handle non-finite values.
Results may differ from the reference program's by a relative error of at most 0.0003.
Values sent between devices are 32-bit elements; how exact they have to be, the bound alone decides.
No kernel may reach another device: no remote copies, remote signals or barrier semaphores. Data moves between devices by JAX's collectives and lax.ppermute only.
A program may use at most 64 MiB of HBM per device.

```python
import math
import jax
import jax.numpy as jnp
from jax import lax

OWN = 2
BR = 128
LB = 6
REACH = 3
NC = 32
PADS = 64
ITERS = 2
NI = 768
NBLK = 32
GROWS = 4096
N_BOARD = 2
N_SUB = 16


def draw_rhs(key, part):
    first = jax.random.fold_in(key, 0)
    third = jax.random.fold_in(key, 2)
    fourth = jax.random.fold_in(key, 3)
    rows = jnp.arange(GROWS, dtype=jnp.float32)
    ramp = 1.0 + 2.0 * rows / max(GROWS - 1, 1)
    rough = jnp.exp(jax.random.uniform(third, (N_BOARD, 1, GROWS), jnp.float32, -0.55, 0.55))
    case_scale = jnp.exp(jax.random.uniform(fourth, (1, NC, 1), jnp.float32, math.log(0.3), math.log(3.0)))
    base = jnp.clip(jax.random.normal(first, (N_BOARD, NC, GROWS), jnp.float32), -6.0, 6.0)
    return (base * ramp[None, None, :] * rough * case_scale).astype(jnp.float32)


def draw_schur(key, part):
    count = N_BOARD * N_SUB
    first, second = jax.random.split(key, 2)
    raw = jax.random.uniform(first, (count, NI, NI), jnp.float32, -1.7320508, 1.7320508)
    mixed = (raw + jnp.swapaxes(raw, 1, 2)) * (0.45 / math.sqrt(2.0 * NI))
    diagonal = jax.random.uniform(second, (count, NI), jnp.float32, 1.5, 3.0)
    rows = jnp.arange(NI, dtype=jnp.int32)
    on_diag = (rows[:, None] == rows[None, :]).astype(jnp.float32)
    matrix = mixed + on_diag[None, :, :] * diagonal[:, :, None]
    return matrix.reshape(N_BOARD, N_SUB * NI, NI).astype(jnp.float32)


def draw_block_list(key, part):
    count = N_BOARD * N_SUB
    domain = jnp.arange(count, dtype=jnp.int32) % N_SUB
    blocks = jnp.arange(NBLK, dtype=jnp.int32)
    owner = blocks // OWN
    distance = jnp.abs(owner[None, :] - domain[:, None])
    raw = jax.random.randint(jax.random.fold_in(key, 11), (count, NBLK), 0, 1 << 16)
    score = raw * NBLK + blocks[None, :]
    score = jnp.where(distance == 0, (1 << 26) + blocks[None, :], score)
    score = jnp.where(distance <= REACH, score, -1 - blocks[None, :])
    chosen = jax.lax.top_k(score, LB)[1].astype(jnp.int32)
    chosen = jnp.sort(chosen, axis=1)
    return chosen.reshape(N_BOARD, N_SUB * LB)


def draw_pad_rows(key, part):
    count = N_BOARD * N_SUB
    owned = OWN * BR
    rows = jnp.arange(owned, dtype=jnp.int32)
    raw = jax.random.randint(jax.random.fold_in(key, 23), (count, owned), 0, 1 << 16)
    score = raw * owned + rows[None, :]
    ends = jnp.logical_or(rows == 0, rows == owned - 1)
    score = jnp.where(ends[None, :], (1 << 28) + rows[None, :], score)
    chosen = jax.lax.top_k(score, PADS)[1].astype(jnp.int32)
    chosen = jnp.sort(chosen, axis=1)
    return chosen.reshape(N_BOARD, N_SUB * PADS)


def block_scale(stream_key, shape, cuts, least, top_value):
    def one(position, blocks):
        steps = jax.random.uniform(jax.random.fold_in(jax.random.fold_in(stream_key, 6), position), (blocks,), jnp.float32, least / len(cuts), top_value / len(cuts))
        return jnp.repeat(jnp.exp(steps), shape[position] // blocks).reshape((-1,) + (1,) * (len(shape) - position - 1))

    loudness = one(*cuts[0])
    for cut in cuts[1:]:
        loudness = loudness * one(*cut)
    return loudness


def setup_inputs(seed: int = 0) -> dict:
    key_of = jax.random.split(jax.random.key(seed), 8)
    rhs = draw_rhs(jax.random.fold_in(key_of[7], 71), 0)
    schur = draw_schur(jax.random.fold_in(key_of[7], 71), 0)
    block_list = draw_block_list(jax.random.fold_in(key_of[7], 71), 0)
    pad_rows = draw_pad_rows(jax.random.fold_in(key_of[7], 71), 0)
    pad_cond = jnp.clip(jnp.exp(math.log(2.0) - 1.3862944 * jax.random.uniform(key_of[4], (N_BOARD, N_SUB * PADS), jnp.float32) ** block_scale(key_of[4], (N_BOARD, N_SUB * PADS), ((0, 2), (1, 16)), -0.2, 0.2)), 0.5, 2.0)
    sink = jnp.clip(jnp.exp(math.log(2.0) - 2.3025851 * jax.random.uniform(key_of[5], (N_BOARD, GROWS), jnp.float32) ** block_scale(key_of[5], (N_BOARD, GROWS), ((0, 2), (1, 16)), -0.2, 0.2)), 0.2, 2.0)
    precond = jnp.clip(jnp.exp(math.log(1.0) - 1.2039728 * jax.random.uniform(key_of[6], (N_BOARD, GROWS), jnp.float32) ** block_scale(key_of[6], (N_BOARD, GROWS), ((0, 2), (1, 16)), -0.2, 0.2)), 0.3, 1.0)
    return dict(rhs=rhs, schur=schur, block_list=block_list, pad_rows=pad_rows, pad_cond=pad_cond, sink=sink, precond=precond)


def apply_operator(direction, schur, block_list, pad_rows, pad_cond, sink):
    mats = schur.reshape(N_BOARD * N_SUB, NI, NI)
    lists = block_list.reshape(N_BOARD * N_SUB, LB)
    start = jnp.zeros((N_BOARD, NC, NBLK, BR), jnp.float32)

    def one_domain(total, item):
        number, matrix, block_ids = item
        board_id = number // N_SUB
        blocks = lax.dynamic_index_in_dim(direction, board_id, 0, keepdims=False).reshape(NC, NBLK, BR)
        picked = jnp.take(blocks, block_ids, axis=1).reshape(NC, NI)
        product = jnp.dot(picked, matrix, precision=lax.Precision.HIGHEST).reshape(NC, LB, BR)
        current = lax.dynamic_index_in_dim(total, board_id, 0, keepdims=False)
        current = current.at[:, block_ids].add(product)
        return lax.dynamic_update_index_in_dim(total, current, board_id, 0), None

    numbers = jnp.arange(N_BOARD * N_SUB, dtype=jnp.int32)
    total, unused = lax.scan(one_domain, start, (numbers, mats, lists))
    result = total.reshape(N_BOARD, NC, GROWS)
    offsets = (jnp.arange(N_SUB, dtype=jnp.int32) * (OWN * BR))[None, :, None]
    rows_all = (pad_rows.reshape(N_BOARD, N_SUB, PADS) + offsets).reshape(N_BOARD, N_SUB * PADS)
    pad_values = jnp.take_along_axis(direction, rows_all[:, None, :], axis=2)
    partner = jnp.arange(N_BOARD, dtype=jnp.int32) ^ 1
    mean_cond = 0.5 * (pad_cond + pad_cond[partner])
    coupling = mean_cond[:, None, :] * (pad_values - pad_values[partner])
    board_ids = jnp.arange(N_BOARD, dtype=jnp.int32)[:, None, None]
    case_ids = jnp.arange(NC, dtype=jnp.int32)[None, :, None]
    result = result.at[board_ids, case_ids, rows_all[:, None, :]].add(coupling)
    return result + sink[:, None, :] * direction


def case_sums(left, right):
    return jnp.sum(left * right, axis=(0, 2))


def reference(rhs, schur, block_list, pad_rows, pad_cond, sink, precond):
    scaling = precond[:, None, :]
    solution = jnp.zeros_like(rhs)
    residual = rhs
    precon = scaling * residual
    direction = precon
    norm_now = case_sums(residual, precon)
    for iteration in range(ITERS):
        image = apply_operator(direction, schur, block_list, pad_rows, pad_cond, sink)
        alpha = norm_now / case_sums(direction, image)
        solution = solution + alpha[None, :, None] * direction
        residual = residual - alpha[None, :, None] * image
        if iteration < ITERS - 1:
            precon = scaling * residual
            fresh = case_sums(residual, precon)
            direction = precon + (fresh / norm_now)[None, :, None] * direction
            norm_now = fresh
    return solution, residual
```

```python
import jax
import jax.numpy as jnp
from jax import lax
from jax.experimental import pallas as pl
from jax.experimental.pallas import tpu as pltpu
from jax.sharding import PartitionSpec as P

BR = 128
REACH = 3
ITERS = 2
F32 = jnp.float32
HALF = jnp.bfloat16
barrier = lax.optimization_barrier


def passed_along(value, axis, steps):
    count = lax.axis_size(axis)
    leading, last = (max(0, -steps), min(count, count - steps))
    return lax.ppermute(value, axis, [(source, source + steps) for source in range(leading, last)])


def case_sums(left, right):
    return jnp.sum(left * right, axis=1)


def step_by_step(right_side, matrix, block_ids, pad_local, conduct, sink_rows, scaling):
    cases, owned_rows = right_side.shape
    blocks_owned = owned_rows // BR
    inner = matrix.shape[0]
    touched = block_ids.shape[0]
    across = [(i, i ^ 1) for i in range(lax.axis_size("board"))]
    shifted_ids = block_ids - (lax.axis_index("sub") - REACH) * blocks_owned
    solution = jnp.zeros_like(right_side)
    residual = right_side
    precon = scaling * residual
    direction = precon
    norm_now = lax.psum(case_sums(residual, precon), ("board", "sub"))
    for iteration in range(ITERS):
        segments = [
            direction if offset == 0 else passed_along(direction, "sub", -offset)
            for offset in range(-REACH, REACH + 1)
        ]
        apply_blocks = jnp.concatenate(segments, axis=1).reshape(cases, -1, BR)
        picked = jnp.take(apply_blocks, shifted_ids, axis=1).reshape(cases, inner)
        product = jnp.dot(picked, matrix, precision=lax.Precision.HIGHEST)
        partial_value = (
            jnp.zeros(apply_blocks.shape, F32).at[:, shifted_ids].add(product.reshape(cases, touched, BR))
        )
        pieces = partial_value.reshape(cases, 2 * REACH + 1, owned_rows)
        result = pieces[:, REACH]
        for offset in range(-REACH, REACH + 1):
            if offset != 0:
                result = result + passed_along(pieces[:, REACH + offset], "sub", offset)
        pad_values = jnp.take(direction, pad_local, axis=1)
        other_values = lax.ppermute(pad_values, "board", across)
        mean_cond = 0.5 * (conduct + lax.ppermute(conduct, "board", across))
        result = result.at[:, pad_local].add(mean_cond[None, :] * (pad_values - other_values))
        image = result + sink_rows * direction
        alpha = norm_now / lax.psum(case_sums(direction, image), ("board", "sub"))
        solution = solution + alpha[:, None] * direction
        residual = residual - alpha[:, None] * image
        if iteration < ITERS - 1:
            precon = scaling * residual
            fresh = lax.psum(case_sums(residual, precon), ("board", "sub"))
            direction = precon + (fresh / norm_now)[:, None] * direction
            norm_now = fresh
    return solution, residual


def climb(count, step):
    pairs = []
    for source in range(count):
        chip, core = divmod(source, 2)
        target = chip - step if core else chip + step
        inside = 0 <= target < count // 2
        pairs.append((source, target * 2 + core if inside else source ^ 1))
    return pairs


def leap(count):
    pairs = []
    for source in range(count):
        chip, core = divmod(source, 2)
        target = chip + 2 if core else chip - 2
        if 0 <= target < count // 2:
            pairs.append((source, target * 2 + 1 - core))
        else:
            pairs.append((source, source ^ 2))
    return pairs


def turned(pairs):
    return [(target, source) for source, target in pairs]


def thirds(value):
    high = value.astype(HALF)
    rest = value - high.astype(F32)
    middle = rest.astype(HALF)
    return high, middle, (rest - middle.astype(F32)).astype(HALF)


def dot(left, right):
    return jnp.dot(left, right, preferred_element_type=F32)


def times_ones(value, ones, turn):
    rows = value.shape[0]
    parts = jnp.concatenate(thirds(value))
    if turn:
        out = lax.dot_general(parts, ones, (((1,), (1,)), ((), ())), preferred_element_type=F32)
    else:
        out = dot(parts, ones)
    return out[:rows] + (out[rows : 2 * rows] + out[2 * rows :])


def product_of(value, high, middle, low):
    rows = value.shape[0]
    one, two, three = thirds(value)
    first = dot(jnp.concatenate([one, two, three]), high[...])
    second = dot(jnp.concatenate([one, two]), middle[...])
    small = first[2 * rows :] + second[rows:] + dot(one, low[...])
    return (small + (first[rows : 2 * rows] + second[:rows])) + first[:rows]


def wide(pair):
    return jnp.concatenate([pair[0], pair[1]], axis=1)


def put_wide(ref, start, value):
    ref[start] = value[:, :BR]
    ref[start + 1] = value[:, BR:]


def lanes_of(cases, slot):
    lane = lax.broadcasted_iota(jnp.int32, (cases, BR), 1)
    return lane == lax.broadcasted_iota(jnp.int32, (cases, BR), 0) + slot * cases


def as_row(column, slot):
    return jnp.sum(jnp.where(lanes_of(column.shape[0], slot), column, 0.0), axis=0, keepdims=True)


def as_column(row, slot, cases):
    return jnp.sum(jnp.where(lanes_of(cases, slot), row, 0.0), axis=1, keepdims=True)


def begin_kernel(rhs, precond, sink, pads, cond, rhs_out, rows_out, z_out, ones_out, pads_out, pad_at, cond_at, sems):
    copies = [
        pltpu.make_async_copy(rhs, rhs_out, sems.at[0]),
        pltpu.make_async_copy(precond, rows_out.at[0], sems.at[1]),
        pltpu.make_async_copy(sink, rows_out.at[1], sems.at[2]),
        pltpu.make_async_copy(pads, pad_at, sems.at[3]),
        pltpu.make_async_copy(cond, cond_at, sems.at[4]),
    ]
    for copy in copies:
        copy.start()
    for copy in copies:
        copy.wait()
    z = rows_out[0] * rhs_out[...]
    cases, owned = z.shape
    put_wide(z_out, 0, z)
    count = pad_at.shape[1]
    here = lax.broadcasted_iota(jnp.int32, (owned, count), 0)
    ones = (here == pad_at[...]).astype(F32).astype(HALF)
    ones_out[...] = ones
    pads_out[...] = jnp.zeros_like(pads_out)
    pads_out[:cases, :count] = times_ones(z, ones, False)
    pads_out[cases : cases + 1, :count] = cond_at[...]


def prepare_kernel(schur, blocks, high, middle, low, places, held, listed, sems):
    chunk = held.shape[0] // (sems.shape[0] - 1)
    copies = []
    for i in range(sems.shape[0] - 1):
        rows = slice(i * chunk, (i + 1) * chunk)
        copies.append(pltpu.make_async_copy(schur.at[rows], held.at[rows], sems.at[i]))
    lists = pltpu.make_async_copy(blocks, listed, sems.at[sems.shape[0] - 1])
    lists.start()
    for copy in copies:
        copy.start()
    position = lax.axis_index("sub")
    chip, core = position // 2, lax.rem(position, 2)
    above, below = lax.axis_size("sub") // 2 - 1 - chip, chip
    lists.wait()
    touched = listed.shape[1]
    offset = listed[...] // 2 - position
    mirrored = jnp.where(core == 0, offset, -offset)
    place = jnp.where(mirrored == 2, 6, jnp.where(mirrored == 3, 5, mirrored + REACH))
    place = place * 2 + lax.rem(listed[...], 2)
    spots = 2 * (2 * REACH + 1)
    for i in range(touched):
        here = jnp.broadcast_to(place[:, i : i + 1], places.shape[1:])
        for j in range(spots):
            places[i * spots + j] = (here == j).astype(F32)
    near = jnp.where(core == 0, above, below) >= 1
    far = jnp.where(core == 0, below, above) >= 2
    for i, sender in enumerate((near, far)):
        places[touched * spots + i] = jnp.full(places.shape[1:], sender.astype(F32))
    for i, copy in enumerate(copies):
        rows = slice(i * chunk, (i + 1) * chunk)
        copy.wait()
        high[rows], middle[rows], low[rows] = thirds(held[rows])


def product_kernel(first, places, high, middle, low, p2, p1, own, a, b, there, conds, mine, ones, rows, *rest):
    if first:
        back, to_p1, to_p2, kept = rest
    else:
        sums, back, to_p1, to_p2, kept, sums_out = rest
    touched = high.shape[0] // BR
    cases = own.shape[1]
    spots = 2 * (2 * REACH + 1)
    held = [p2[0], p2[1], p1[0], p1[1], p1[2], p1[3], own[0], own[1], a[0], a[1], b[0], b[1], b[2], b[3]]

    def spot(i, j):
        return jnp.concatenate([places[i * spots + j]] * (cases // 8))

    picked = []
    for i in range(touched):
        total = spot(i, 0) * held[0]
        for j in range(1, spots):
            total = total + spot(i, j) * held[j]
        picked.append(total)
    picked = jnp.concatenate(picked, axis=1)
    product = product_of(picked, high, middle, low)

    def landed(j):
        total = spot(0, j) * product[:, :BR]
        for i in range(1, touched):
            total = total + spot(i, j) * product[:, i * BR : (i + 1) * BR]
        return total

    for j in range(2):
        to_p2[j] = landed(j)
    for j in range(4):
        back[j] = landed(10 + j)
        to_p1[j] = landed(2 + j)
    kept[2] = landed(8)
    kept[3] = landed(9)
    count = ones.shape[1]
    mean_cond = 0.5 * (mine[cases : cases + 8, :count] + conds[cases : cases + 8, :count])
    spread = jnp.concatenate([mean_cond[:1] * there[:cases, :count], mean_cond])
    spread = times_ones(spread, ones[...], True)
    here = wide(own)
    local = (rows[1] + spread[cases : cases + 1]) * here - spread[:cases]
    kept[0] = landed(6) + local[:, :BR]
    kept[1] = landed(7) + local[:, BR:]
    if not first:
        energy = jnp.sum(picked * product, axis=1, keepdims=True) + jnp.sum(here * local, axis=1, keepdims=True)
        total = sums[...] + as_row(energy, 3)
        sums_out[...] = jnp.broadcast_to(total[None], sums_out.shape)


def gather_parts(places, kept, from_p1, from_p2):
    near, far = [
        jnp.concatenate([places[places.shape[0] - 2 + i]] * (kept.shape[1] // 8))[None] for i in range(2)
    ]
    one = from_p1[...] * near
    return kept[0:2] + one[0:2] + from_p2[...] * far, kept[2:4] + one[2:4]


def part_kernel(places, kept, from_p1, from_p2, rows, part):
    mine, other = gather_parts(places, kept, from_p1, from_p2)
    part[0:2] = mine
    part[2:4] = other
    part[4] = jnp.zeros(part.shape[1:], F32)
    part[4, 0:1] = rows[0, :, :BR]
    part[4, 1:2] = rows[0, :, BR:]


def turn_kernel(part, there, rhs, z, rows, ones, image_out, both_out, own_out, pads_out, sums_out):
    image = wide(part[0:2] + there[2:4])
    other = part[2:4] + there[0:2]
    image_out[...] = image
    scaled = rows[0] * image
    put_wide(both_out, 0, scaled)
    put_wide(own_out, 0, scaled)
    both_out[2] = there[4, 0:1] * other[0]
    both_out[3] = there[4, 1:2] * other[1]
    count = ones.shape[1]
    pads_out[...] = jnp.zeros_like(pads_out)
    pads_out[:, :count] = times_ones(scaled, ones[...], False)
    start = wide(z)
    one = jnp.sum(rhs[...] * start, axis=1, keepdims=True)
    two = jnp.sum(start * image, axis=1, keepdims=True)
    three = jnp.sum(image * scaled, axis=1, keepdims=True)
    sums_out[...] = as_row(one, 0) + as_row(two, 1) + as_row(three, 2)


def last_part_kernel(places, kept, from_p1, from_p2, mine_out, other_out):
    mine_out[...], other_out[...] = gather_parts(places, kept, from_p1, from_p2)


def steps_kernel(sums, steps, fine):
    cases = steps.shape[1]
    total = jnp.sum(sums[...], axis=0)
    norm, curve, cross, energy = [as_column(total, slot, cases) for slot in range(4)]
    alpha = norm / curve
    fresh = alpha * alpha * cross - norm
    grown = 1.0 + fresh / norm
    terms = [grown * grown * curve, 2.0 * alpha * grown * cross, alpha * alpha * energy]
    bend = terms[0] - terms[1] + terms[2]
    good = (norm > 1e-30) & (energy < 1e30) & (cross < 1e30) & (curve > 0.0) & (fresh > 0.02 * norm)
    good = good & (bend > 0.004 * (terms[0] + terms[1] + terms[2]))
    fine[0, 0] = jnp.sum(jnp.where(good, 1, 0))
    for i, value in enumerate((alpha, grown, fresh / bend)):
        steps[i] = jnp.broadcast_to(value, steps.shape[1:])


def end_kernel(rhs, z, image, scaled, mine, there, steps, solution, residual):
    alpha, grown, step = [wide([steps[i], steps[i]]) for i in range(3)]
    start = wide(z)
    direction = grown * start - alpha * wide(scaled)
    solution[...] = alpha * start + step * direction
    second = wide(mine[...] + there[...])
    residual[...] = rhs[...] - alpha * image[...] - step * (grown * image[...] - alpha * second)


def call(kernel, outs, *operands, scratch=(), far=(), scalar=()):
    def space(outside, i, smem=()):
        return pl.BlockSpec(memory_space=pl.ANY if i in outside else pltpu.SMEM if i in smem else pltpu.VMEM)

    return pl.pallas_call(
        kernel,
        in_specs=[space(far, i) for i in range(len(operands))],
        out_specs=[space((), i, scalar) for i in range(len(outs))],
        out_shape=[jax.ShapeDtypeStruct(shape, kind) for shape, kind in outs],
        scratch_shapes=list(scratch),
        compiler_params=pltpu.CompilerParams(vmem_limit_bytes=32 * 1024 * 1024),
    )(*operands)


def on_device(rhs, schur, block_list, pad_rows, pad_cond, sink, precond):
    matrix = schur[0]
    cases, owned = rhs.shape[1:]
    inner = matrix.shape[0]
    blocks = owned // BR
    touched = inner // BR
    count = lax.axis_size("sub")
    everyone = count * lax.axis_size("board")
    pads = pad_rows.shape[1]
    swap = [(i, i ^ 1) for i in range(count)]
    across = [(i, i ^ 1) for i in range(lax.axis_size("board"))]
    near, far = climb(count, 1), leap(count)
    pair = ((blocks, cases, BR), F32)
    both = ((2 * blocks, cases, BR), F32)
    row = ((1, BR), F32)
    full = ((cases, owned), F32)
    semaphores = pltpu.SemaphoreType.DMA

    right_side, rows, z, ones, pads_sent = call(
        begin_kernel,
        [full, ((2, 1, owned), F32), pair, ((owned, pads), HALF), ((cases + 8, BR), F32)],
        rhs[0], precond, sink, pad_rows, pad_cond,
        far=range(5),
        scratch=[pltpu.VMEM((1, pads), jnp.int32), pltpu.VMEM((1, pads), F32), semaphores((5,))],
    )
    chunks = 6
    spots = 2 * (2 * REACH + 1)
    high, middle, low, places = call(
        prepare_kernel,
        [((inner, inner), HALF)] * 3 + [((touched * spots + 2, 8, BR), F32)],
        matrix, block_list,
        far=range(2),
        scratch=[pltpu.VMEM((inner, inner), F32), pltpu.VMEM((1, touched), jnp.int32), semaphores((chunks + 1,))],
    )

    def product(first, *operands):
        return call(
            lambda *refs: product_kernel(first, *refs),
            [both, both, pair, both] + ([] if first else [((everyone, 1, BR), F32)]),
            places, high, middle, low, *operands,
        )

    def collect(back, to_p1, to_p2):
        from_p2 = lax.ppermute(to_p2, "sub", far)
        to_p1 = to_p1 + lax.ppermute(back, "sub", swap)
        return to_p1, from_p2

    other = lax.ppermute(z, "sub", swap)
    p2 = lax.ppermute(z, "sub", far)
    conds = lax.ppermute(pads_sent, "board", across)
    p1 = lax.ppermute(jnp.concatenate([z, other]), "sub", near)
    p1, p2, conds = barrier((p1, p2, conds))
    b = lax.ppermute(p1, "sub", swap)
    back, to_p1, to_p2, kept = product(True, p2, p1, z, other, b, conds, conds, pads_sent, ones, rows)
    to_p1, from_p2 = collect(back, to_p1, to_p2)
    from_p1 = lax.ppermute(to_p1, "sub", turned(near))
    (part,) = call(part_kernel, [((2 * blocks + 1, cases, BR), F32)], places, kept, from_p1, from_p2, rows)
    part_there = lax.ppermute(part, "sub", swap)
    image, four, own, values, sums = call(
        turn_kernel, [full, both, pair, ((cases, BR), F32), row], part, part_there, right_side, z, rows, ones
    )
    p1 = lax.ppermute(four, "sub", near)
    p2 = lax.ppermute(own, "sub", far)
    there = lax.ppermute(values, "board", across)
    p1, p2, there = barrier((p1, p2, there))
    b = lax.ppermute(p1, "sub", swap)
    back, to_p1, to_p2, kept, sums = product(
        False, p2, p1, own, four[blocks:], b, there, conds, pads_sent, ones, rows, sums
    )
    to_p1, from_p2 = collect(back, to_p1, to_p2)
    to_p1, sums = barrier((to_p1, sums))
    from_p1 = lax.ppermute(to_p1, "sub", turned(near))
    all_sums = lax.all_to_all(sums, ("board", "sub"), 0, 0)
    from_p1, from_p2, all_sums = barrier((from_p1, from_p2, all_sums))
    mine, to_other = call(last_part_kernel, [pair, pair], places, kept, from_p1, from_p2)
    there = lax.ppermute(to_other, "sub", swap)
    steps, fine = call(
        steps_kernel, [((3, cases, BR), F32), ((1, 1), jnp.int32)], all_sums, scalar=(1,)
    )
    solution, residual = lax.cond(
        fine[0, 0] == cases,
        lambda: tuple(call(end_kernel, [full, full], right_side, z, image, own, mine, there, steps)),
        lambda: step_by_step(rhs[0], matrix, block_list[0], pad_rows[0], pad_cond[0], sink, precond),
    )
    return (solution[None], residual[None])


def solution(mesh):
    in_specs = (
        P("board", None, "sub"),
        P("board", "sub", None),
        P("board", "sub"),
        P("board", "sub"),
        P("board", "sub"),
        P("board", "sub"),
        P("board", "sub"),
    )
    out_specs = (P("board", None, "sub"), P("board", None, "sub"))
    return jax.shard_map(
        on_device, mesh=mesh, in_specs=in_specs, out_specs=out_specs, check_vma=False
    )
```

```python
import jax
import jax.numpy as jnp
from jax import lax
from jax.experimental import pallas as pl
from jax.experimental.pallas import tpu as pltpu
from jax.sharding import PartitionSpec as P

BR = 128
REACH = 3
ITERS = 2
F32 = jnp.float32
HALF = jnp.bfloat16
barrier = lax.optimization_barrier


def passed_along(value, axis, steps):
    count = lax.axis_size(axis)
    leading, last = (max(0, -steps), min(count, count - steps))
    return lax.ppermute(value, axis, [(source, source + steps) for source in range(leading, last)])


def case_sums(left, right):
    return jnp.sum(left * right, axis=1)


def step_by_step(right_side, matrix, block_ids, pad_local, conduct, sink_rows, scaling):
    cases, owned_rows = right_side.shape
    blocks_owned = owned_rows // BR
    inner = matrix.shape[0]
    touched = block_ids.shape[0]
    across = [(i, i ^ 1) for i in range(lax.axis_size("board"))]
    shifted_ids = block_ids - (lax.axis_index("sub") - REACH) * blocks_owned
    solution = jnp.zeros_like(right_side)
    residual = right_side
    precon = scaling * residual
    direction = precon
    norm_now = lax.psum(case_sums(residual, precon), ("board", "sub"))
    for iteration in range(ITERS):
        segments = [
            direction if offset == 0 else passed_along(direction, "sub", -offset)
            for offset in range(-REACH, REACH + 1)
        ]
        apply_blocks = jnp.concatenate(segments, axis=1).reshape(cases, -1, BR)
        picked = jnp.take(apply_blocks, shifted_ids, axis=1).reshape(cases, inner)
        product = jnp.dot(picked, matrix, precision=lax.Precision.HIGHEST)
        partial_value = (
            jnp.zeros(apply_blocks.shape, F32).at[:, shifted_ids].add(product.reshape(cases, touched, BR))
        )
        pieces = partial_value.reshape(cases, 2 * REACH + 1, owned_rows)
        result = pieces[:, REACH]
        for offset in range(-REACH, REACH + 1):
            if offset != 0:
                result = result + passed_along(pieces[:, REACH + offset], "sub", offset)
        pad_values = jnp.take(direction, pad_local, axis=1)
        other_values = lax.ppermute(pad_values, "board", across)
        mean_cond = 0.5 * (conduct + lax.ppermute(conduct, "board", across))
        result = result.at[:, pad_local].add(mean_cond[None, :] * (pad_values - other_values))
        image = result + sink_rows * direction
        alpha = norm_now / lax.psum(case_sums(direction, image), ("board", "sub"))
        solution = solution + alpha[:, None] * direction
        residual = residual - alpha[:, None] * image
        if iteration < ITERS - 1:
            precon = scaling * residual
            fresh = lax.psum(case_sums(residual, precon), ("board", "sub"))
            direction = precon + (fresh / norm_now)[:, None] * direction
            norm_now = fresh
    return solution, residual


def climb(count, step):
    pairs = []
    for source in range(count):
        chip, core = divmod(source, 2)
        target = chip - step if core else chip + step
        inside = 0 <= target < count // 2
        pairs.append((source, target * 2 + core if inside else source ^ 1))
    return pairs


def leap(count):
    pairs = []
    for source in range(count):
        chip, core = divmod(source, 2)
        target = chip + 2 if core else chip - 2
        if 0 <= target < count // 2:
            pairs.append((source, target * 2 + 1 - core))
        else:
            pairs.append((source, source ^ 2))
    return pairs


def turned(pairs):
    return [(target, source) for source, target in pairs]


def thirds(value):
    high = value.astype(HALF)
    rest = value - high.astype(F32)
    middle = rest.astype(HALF)
    return high, middle, (rest - middle.astype(F32)).astype(HALF)


def dot(left, right):
    return jnp.dot(left, right, preferred_element_type=F32)


def times_ones(value, ones, turn):
    rows = value.shape[0]
    parts = jnp.concatenate(thirds(value))
    if turn:
        out = lax.dot_general(parts, ones, (((1,), (1,)), ((), ())), preferred_element_type=F32)
    else:
        out = dot(parts, ones)
    return out[:rows] + (out[rows : 2 * rows] + out[2 * rows :])


def product_of(value, high, middle, low):
    rows = value.shape[0]
    one, two, three = thirds(value)
    first = dot(jnp.concatenate([one, two, three]), high[...])
    second = dot(jnp.concatenate([one, two]), middle[...])
    small = first[2 * rows :] + second[rows:] + dot(one, low[...])
    return (small + (first[rows : 2 * rows] + second[:rows])) + first[:rows]


def wide(pair):
    return jnp.concatenate([pair[0], pair[1]], axis=1)


def put_wide(ref, start, value):
    ref[start] = value[:, :BR]
    ref[start + 1] = value[:, BR:]


def lanes_of(cases, slot):
    lane = lax.broadcasted_iota(jnp.int32, (cases, BR), 1)
    return lane == lax.broadcasted_iota(jnp.int32, (cases, BR), 0) + slot * cases


def as_row(column, slot):
    return jnp.sum(jnp.where(lanes_of(column.shape[0], slot), column, 0.0), axis=0, keepdims=True)


def as_column(row, slot, cases):
    return jnp.sum(jnp.where(lanes_of(cases, slot), row, 0.0), axis=1, keepdims=True)


def begin_kernel(rhs, precond, sink, pads, cond, rhs_out, rows_out, z_out, ones_out, pads_out, pad_at, cond_at, sems):
    copies = [
        pltpu.make_async_copy(rhs, rhs_out, sems.at[0]),
        pltpu.make_async_copy(precond, rows_out.at[0], sems.at[1]),
        pltpu.make_async_copy(sink, rows_out.at[1], sems.at[2]),
        pltpu.make_async_copy(pads, pad_at, sems.at[3]),
        pltpu.make_async_copy(cond, cond_at, sems.at[4]),
    ]
    for copy in copies:
        copy.start()
    for copy in copies:
        copy.wait()
    z = rows_out[0] * rhs_out[...]
    cases, owned = z.shape
    put_wide(z_out, 0, z)
    count = pad_at.shape[1]
    here = lax.broadcasted_iota(jnp.int32, (owned, count), 0)
    ones = (here == pad_at[...]).astype(F32).astype(HALF)
    ones_out[...] = ones
    pads_out[...] = jnp.zeros_like(pads_out)
    pads_out[:cases, :count] = times_ones(z, ones, False)
    pads_out[cases : cases + 1, :count] = cond_at[...]


def prepare_kernel(schur, blocks, high, middle, low, places, held, listed, sems):
    chunk = held.shape[0] // (sems.shape[0] - 1)
    copies = []
    for i in range(sems.shape[0] - 1):
        rows = slice(i * chunk, (i + 1) * chunk)
        copies.append(pltpu.make_async_copy(schur.at[rows], held.at[rows], sems.at[i]))
    lists = pltpu.make_async_copy(blocks, listed, sems.at[sems.shape[0] - 1])
    lists.start()
    for copy in copies:
        copy.start()
    position = lax.axis_index("sub")
    chip, core = position // 2, lax.rem(position, 2)
    above, below = lax.axis_size("sub") // 2 - 1 - chip, chip
    lists.wait()
    touched = listed.shape[1]
    offset = listed[...] // 2 - position
    mirrored = jnp.where(core == 0, offset, -offset)
    place = jnp.where(mirrored == 2, 6, jnp.where(mirrored == 3, 5, mirrored + REACH))
    place = place * 2 + lax.rem(listed[...], 2)
    spots = 2 * (2 * REACH + 1)
    for i in range(touched):
        here = jnp.broadcast_to(place[:, i : i + 1], places.shape[1:])
        for j in range(spots):
            places[i * spots + j] = (here == j).astype(F32)
    near = jnp.where(core == 0, above, below) >= 1
    far = jnp.where(core == 0, below, above) >= 2
    for i, sender in enumerate((near, far)):
        places[touched * spots + i] = jnp.full(places.shape[1:], sender.astype(F32))
    for i, copy in enumerate(copies):
        rows = slice(i * chunk, (i + 1) * chunk)
        copy.wait()
        high[rows], middle[rows], low[rows] = thirds(held[rows])


def product_kernel(first, places, high, middle, low, p2, p1, own, a, b, there, conds, mine, ones, rows, *rest):
    if first:
        back, to_p1, to_p2, kept = rest
    else:
        sums, back, to_p1, to_p2, kept, sums_out = rest
    touched = high.shape[0] // BR
    cases = own.shape[1]
    spots = 2 * (2 * REACH + 1)
    held = [p2[0], p2[1], p1[0], p1[1], p1[2], p1[3], own[0], own[1], a[0], a[1], b[0], b[1], b[2], b[3]]

    def spot(i, j):
        return jnp.concatenate([places[i * spots + j]] * (cases // 8))

    picked = []
    for i in range(touched):
        total = spot(i, 0) * held[0]
        for j in range(1, spots):
            total = total + spot(i, j) * held[j]
        picked.append(total)
    picked = jnp.concatenate(picked, axis=1)
    product = product_of(picked, high, middle, low)

    def landed(j):
        total = spot(0, j) * product[:, :BR]
        for i in range(1, touched):
            total = total + spot(i, j) * product[:, i * BR : (i + 1) * BR]
        return total

    for j in range(2):
        to_p2[j] = landed(j)
    for j in range(4):
        back[j] = landed(10 + j)
        to_p1[j] = landed(2 + j)
    kept[2] = landed(8)
    kept[3] = landed(9)
    count = ones.shape[1]
    mean_cond = 0.5 * (mine[cases : cases + 8, :count] + conds[cases : cases + 8, :count])
    spread = jnp.concatenate([mean_cond[:1] * there[:cases, :count], mean_cond])
    spread = times_ones(spread, ones[...], True)
    here = wide(own)
    local = (rows[1] + spread[cases : cases + 1]) * here - spread[:cases]
    kept[0] = landed(6) + local[:, :BR]
    kept[1] = landed(7) + local[:, BR:]
    if not first:
        energy = jnp.sum(picked * product, axis=1, keepdims=True) + jnp.sum(here * local, axis=1, keepdims=True)
        total = sums[...] + as_row(energy, 3)
        sums_out[...] = jnp.broadcast_to(total[None], sums_out.shape)


def gather_parts(places, kept, from_p1, from_p2):
    near, far = [
        jnp.concatenate([places[places.shape[0] - 2 + i]] * (kept.shape[1] // 8))[None] for i in range(2)
    ]
    one = from_p1[...] * near
    return kept[0:2] + one[0:2] + from_p2[...] * far, kept[2:4] + one[2:4]


def part_kernel(places, kept, from_p1, from_p2, rows, part):
    mine, other = gather_parts(places, kept, from_p1, from_p2)
    part[0:2] = mine
    part[2:4] = other
    part[4] = jnp.zeros(part.shape[1:], F32)
    part[4, 0:1] = rows[0, :, :BR]
    part[4, 1:2] = rows[0, :, BR:]


def turn_kernel(part, there, rhs, z, rows, ones, image_out, both_out, own_out, pads_out, sums_out):
    image = wide(part[0:2] + there[2:4])
    other = part[2:4] + there[0:2]
    image_out[...] = image
    scaled = rows[0] * image
    put_wide(both_out, 0, scaled)
    put_wide(own_out, 0, scaled)
    both_out[2] = there[4, 0:1] * other[0]
    both_out[3] = there[4, 1:2] * other[1]
    count = ones.shape[1]
    pads_out[...] = jnp.zeros_like(pads_out)
    pads_out[:, :count] = times_ones(scaled, ones[...], False)
    start = wide(z)
    one = jnp.sum(rhs[...] * start, axis=1, keepdims=True)
    two = jnp.sum(start * image, axis=1, keepdims=True)
    three = jnp.sum(image * scaled, axis=1, keepdims=True)
    sums_out[...] = as_row(one, 0) + as_row(two, 1) + as_row(three, 2)


def last_part_kernel(places, kept, from_p1, from_p2, mine_out, other_out):
    mine_out[...], other_out[...] = gather_parts(places, kept, from_p1, from_p2)


def steps_kernel(sums, steps):
    cases = steps.shape[1]
    total = jnp.sum(sums[...], axis=0)[:1]
    norm, curve, cross, energy = [as_column(total, slot, cases) for slot in range(4)]
    alpha = norm / curve
    fresh = alpha * alpha * cross - norm
    grown = 1.0 + fresh / norm
    terms = [grown * grown * curve, 2.0 * alpha * grown * cross, alpha * alpha * energy]
    bend = terms[0] - terms[1] + terms[2]
    good = (norm > 1e-30) & (energy < 1e30) & (cross < 1e30) & (curve > 0.0) & (fresh > 0.02 * norm)
    good = good & (bend > 0.004 * (terms[0] + terms[1] + terms[2]))
    good = jnp.where(good, 1.0, 0.0)
    for i, value in enumerate((alpha, grown, fresh / bend, good)):
        steps[i] = jnp.broadcast_to(value, steps.shape[1:])


def end_kernel(rhs, z, image, scaled, mine, there, steps, spare_one, spare_two, solution, residual, sems):
    alpha, grown, step = [wide([steps[i], steps[i]]) for i in range(3)]
    start = wide(z)
    direction = grown * start - alpha * wide(scaled)
    solution[...] = alpha * start + step * direction
    second = wide(mine[...] + there[...])
    residual[...] = rhs[...] - alpha * image[...] - step * (grown * image[...] - alpha * second)

    @pl.when(jnp.min(steps[3]) < 0.5)
    def _():
        copies = [
            pltpu.make_async_copy(spare_one, solution, sems.at[0]),
            pltpu.make_async_copy(spare_two, residual, sems.at[1]),
        ]
        for copy in copies:
            copy.start()
        for copy in copies:
            copy.wait()


def call(kernel, outs, *operands, scratch=(), far=(), far_outs=(), smem=(), smem_outs=(), cost=None):
    def space(outside, scalar, i):
        return pl.BlockSpec(memory_space=pl.ANY if i in outside else pltpu.SMEM if i in scalar else pltpu.VMEM)

    return pl.pallas_call(
        kernel,
        in_specs=[space(far, smem, i) for i in range(len(operands))],
        out_specs=[space(far_outs, smem_outs, i) for i in range(len(outs))],
        out_shape=[jax.ShapeDtypeStruct(shape, kind) for shape, kind in outs],
        scratch_shapes=list(scratch),
        cost_estimate=cost,
        compiler_params=pltpu.CompilerParams(vmem_limit_bytes=32 * 1024 * 1024),
    )(*operands)


def on_device(rhs, schur, block_list, pad_rows, pad_cond, sink, precond):
    matrix = schur[0]
    cases, owned = rhs.shape[1:]
    inner = matrix.shape[0]
    blocks = owned // BR
    touched = inner // BR
    count = lax.axis_size("sub")
    everyone = count * lax.axis_size("board")
    pads = pad_rows.shape[1]
    swap = [(i, i ^ 1) for i in range(count)]
    across = [(i, i ^ 1) for i in range(lax.axis_size("board"))]
    near, far = climb(count, 1), leap(count)
    pair = ((blocks, cases, BR), F32)
    both = ((2 * blocks, cases, BR), F32)
    row = ((1, BR), F32)
    full = ((cases, owned), F32)
    semaphores = pltpu.SemaphoreType.DMA

    right_side, rows, z, ones, pads_sent = call(
        begin_kernel,
        [full, ((2, 1, owned), F32), pair, ((owned, pads), HALF), ((cases + 8, BR), F32)],
        rhs[0], precond, sink, pad_rows, pad_cond,
        far=range(5),
        scratch=[pltpu.VMEM((1, pads), jnp.int32), pltpu.VMEM((1, pads), F32), semaphores((5,))],
    )
    chunks = 6
    spots = 2 * (2 * REACH + 1)
    high, middle, low, places = call(
        prepare_kernel,
        [((inner, inner), HALF)] * 3 + [((touched * spots + 2, 8, BR), F32)],
        matrix, block_list,
        far=range(2),
        scratch=[pltpu.VMEM((inner, inner), F32), pltpu.VMEM((1, touched), jnp.int32), semaphores((chunks + 1,))],
    )

    def product(first, *operands):
        return call(
            lambda *refs: product_kernel(first, *refs),
            [both, both, pair, both] + ([] if first else [((everyone, 8, BR), F32)]),
            places, high, middle, low, *operands,
        )

    def collect(back, to_p1, to_p2):
        from_p2 = lax.ppermute(to_p2, "sub", far)
        to_p1 = to_p1 + lax.ppermute(back, "sub", swap)
        return to_p1, from_p2

    other = lax.ppermute(z, "sub", swap)
    p2 = lax.ppermute(z, "sub", far)
    conds = lax.ppermute(pads_sent, "board", across)
    p1 = lax.ppermute(jnp.concatenate([z, other]), "sub", near)
    p1, p2, conds, high, middle, low, places = barrier((p1, p2, conds, high, middle, low, places))
    b = lax.ppermute(p1, "sub", swap)
    back, to_p1, to_p2, kept = product(True, p2, p1, z, other, b, conds, conds, pads_sent, ones, rows)
    to_p1, from_p2 = collect(back, to_p1, to_p2)
    from_p1 = lax.ppermute(to_p1, "sub", turned(near))
    (part,) = call(part_kernel, [((2 * blocks + 1, cases, BR), F32)], places, kept, from_p1, from_p2, rows)
    part_there = lax.ppermute(part, "sub", swap)
    image, four, own, values, sums = call(
        turn_kernel, [full, both, pair, ((cases, BR), F32), row], part, part_there, right_side, z, rows, ones
    )
    p1 = lax.ppermute(four, "sub", near)
    p2 = lax.ppermute(own, "sub", far)
    there = lax.ppermute(values, "board", across)
    p1, p2, there = barrier((p1, p2, there))
    b = lax.ppermute(p1, "sub", swap)
    back, to_p1, to_p2, kept, sums = product(
        False, p2, p1, own, four[blocks:], b, there, conds, pads_sent, ones, rows, sums
    )
    to_p1, from_p2 = collect(back, to_p1, to_p2)
    from_p1 = lax.ppermute(to_p1, "sub", turned(near))
    all_sums = lax.all_to_all(sums, ("board", "sub"), 0, 0)
    mine, to_other = call(last_part_kernel, [pair, pair], places, kept, from_p1, from_p2)
    there = lax.ppermute(to_other, "sub", swap)
    all_sums, there = barrier((all_sums, there))
    (steps,) = call(steps_kernel, [((4, cases, BR), F32)], all_sums)
    spare = lax.cond(
        jnp.min(steps[3]) > 0.5,
        lambda: tuple(call(lambda *refs: None, [full, full], far_outs=range(2))),
        lambda: step_by_step(rhs[0], matrix, block_list[0], pad_rows[0], pad_cond[0], sink, precond),
    )
    solution, residual = call(
        end_kernel,
        [full, full],
        right_side, z, image, own, mine, there, steps, *spare,
        far=(7, 8), scratch=[semaphores((2,))],
    )
    return (solution[None], residual[None])


def solution(mesh):
    in_specs = (
        P("board", None, "sub"),
        P("board", "sub", None),
        P("board", "sub"),
        P("board", "sub"),
        P("board", "sub"),
        P("board", "sub"),
        P("board", "sub"),
    )
    out_specs = (P("board", None, "sub"), P("board", None, "sub"))
    return jax.shard_map(
        on_device, mesh=mesh, in_specs=in_specs, out_specs=out_specs, check_vma=False
    )
```

```python
import jax
import jax.numpy as jnp
from jax import lax
from jax.experimental import pallas as pl
from jax.experimental.pallas import tpu as pltpu
from jax.sharding import PartitionSpec as P

BR = 128
REACH = 3
F32 = jnp.float32
HALF = jnp.bfloat16
barrier = lax.optimization_barrier


def climb(count, step):
    pairs = []
    for source in range(count):
        chip, core = divmod(source, 2)
        target = chip - step if core else chip + step
        inside = 0 <= target < count // 2
        pairs.append((source, target * 2 + core if inside else source ^ 1))
    return pairs


def leap(count):
    pairs = []
    for source in range(count):
        chip, core = divmod(source, 2)
        target = chip + 2 if core else chip - 2
        if 0 <= target < count // 2:
            pairs.append((source, target * 2 + 1 - core))
        else:
            pairs.append((source, source ^ 2))
    return pairs


def turned(pairs):
    return [(target, source) for source, target in pairs]


def thirds(value):
    high = value.astype(HALF)
    rest = value - high.astype(F32)
    middle = rest.astype(HALF)
    return high, middle, (rest - middle.astype(F32)).astype(HALF)


def dot(left, right):
    return jnp.dot(left, right, preferred_element_type=F32)


def times_ones(value, ones, turn):
    rows = value.shape[0]
    parts = jnp.concatenate(thirds(value))
    if turn:
        out = lax.dot_general(parts, ones, (((1,), (1,)), ((), ())), preferred_element_type=F32)
    else:
        out = dot(parts, ones)
    return out[:rows] + (out[rows : 2 * rows] + out[2 * rows :])


def pad_matrix(pad_rows, owned):
    here = lax.broadcasted_iota(jnp.int32, (owned, pad_rows.shape[1]), 0)
    return (here == pad_rows).astype(F32).astype(HALF)


def product_of(value, high, middle, low):
    rows = value.shape[0]
    one, two, three = thirds(value)
    first = dot(jnp.concatenate([one, two, three]), high[...])
    second = dot(jnp.concatenate([one, two]), middle[...])
    small = first[2 * rows :] + second[rows:] + dot(one, low[...])
    return (small + (first[rows : 2 * rows] + second[:rows])) + first[:rows]


def wide(pair):
    return jnp.concatenate([pair[0], pair[1]], axis=1)


def put_wide(ref, start, value):
    ref[start] = value[:, :BR]
    ref[start + 1] = value[:, BR:]


def lanes_of(cases, slot):
    lane = lax.broadcasted_iota(jnp.int32, (cases, BR), 1)
    return lane == lax.broadcasted_iota(jnp.int32, (cases, BR), 0) + slot * cases


def as_column(row, slot, cases):
    return jnp.sum(jnp.where(lanes_of(cases, slot), row, 0.0), axis=1, keepdims=True)


def begin_kernel(z, pad_rows, pad_cond, ones_out, pads_out):
    cases = z.shape[0]
    owned, count = ones_out.shape
    ones = pad_matrix(pad_rows[...], owned)
    ones_out[...] = ones
    pads_out[...] = jnp.zeros_like(pads_out)
    pads_out[:cases, :count] = times_ones(z[...], ones, False)
    pads_out[cases : cases + 1, :count] = pad_cond[...]
    pads_out[cases + 8 : cases + 9, :count] = pad_rows[...].astype(F32)


def prepare_kernel(schur, blocks, high, middle, low, places, top, held, sems):
    chunk = held.shape[0] // sems.shape[0]
    copies = []
    for i in range(sems.shape[0]):
        rows = slice(i * chunk, (i + 1) * chunk)
        copies.append(pltpu.make_async_copy(schur.at[rows], held.at[rows], sems.at[i]))
    for copy in copies:
        copy.start()
    position = lax.axis_index("sub")
    chip, core = position // 2, lax.rem(position, 2)
    above, below = lax.axis_size("sub") // 2 - 1 - chip, chip
    touched = blocks.shape[1]
    listed = blocks[...]
    offset = listed // 2 - position
    mirrored = jnp.where(core == 0, offset, -offset)
    place = jnp.where(mirrored == 2, 6, jnp.where(mirrored == 3, 5, mirrored + REACH))
    place = place * 2 + lax.rem(listed, 2)
    spots = 2 * (2 * REACH + 1)
    for i in range(touched):
        here = jnp.broadcast_to(place[:, i : i + 1], places.shape[1:])
        for j in range(spots):
            places[i * spots + j] = (here == j).astype(F32)
    near = jnp.where(core == 0, above, below) >= 1
    far = jnp.where(core == 0, below, above) >= 2
    for i, sender in enumerate((near, far)):
        places[touched * spots + i] = jnp.full(places.shape[1:], sender.astype(F32))
    largest = jnp.ones((1, chunk), F32)
    for i, copy in enumerate(copies):
        rows = slice(i * chunk, (i + 1) * chunk)
        copy.wait()
        high[rows], middle[rows], low[rows] = thirds(0.25 * held[rows])
        largest = jnp.maximum(largest, jnp.max(held[rows, rows], axis=0, keepdims=True))
    top[...] = jnp.broadcast_to(jnp.max(largest, axis=1, keepdims=True), top.shape)


def spot(places, i, cases):
    return jnp.concatenate([places[i]] * (cases // 8))


def picked_blocks(places, held, touched):
    cases, spots = held[0].shape[0], len(held)
    picked = []
    for i in range(touched):
        total = spot(places, i * spots, cases) * held[0]
        for j in range(1, spots):
            total = total + spot(places, i * spots + j, cases) * held[j]
        picked.append(total)
    return jnp.concatenate(picked, axis=1)


def landed_blocks(places, product):
    cases, touched = product.shape[0], product.shape[1] // BR
    spots = (places.shape[0] - 2) // touched
    landed = []
    for j in range(spots):
        total = spot(places, j, cases) * product[:, :BR]
        for i in range(1, touched):
            total = total + spot(places, i * spots + j, cases) * product[:, i * BR : (i + 1) * BR]
        landed.append(total)
    return landed


def halves(*values):
    return [value[:, start : start + BR] for value in values for start in (0, BR)]


def held_blocks(p2, p1, own, a, b):
    return [p2[0], p2[1], p1[0], p1[1], p1[2], p1[3], own[0], own[1], a[0], a[1], b[0], b[1], b[2], b[3]]


def mean_of(mine, conds, cases, count):
    return 0.5 * (mine[cases : cases + 1, :count] + conds[cases : cases + 1, :count])


def first_kernel(
    places, high, middle, low, p2, p1, own, a, b, back, to_p1, to_p2, kept, picked_out, product_out
):
    touched = high.shape[0] // BR
    picked = picked_blocks(places, halves(p2, p1[0], p1[1], own, a, b[0], b[1]), touched)
    product = product_of(4.0 * picked, high, middle, low)
    landed = landed_blocks(places, product)
    for j in range(2):
        to_p2[j] = landed[j]
    for j in range(4):
        back[j] = landed[10 + j]
        to_p1[j] = landed[2 + j]
    for j in range(4):
        kept[j] = landed[6 + j]
    picked_out[...] = picked
    product_out[...] = product


def ties_kernel(z, mine, conds, ones, sink, local, jump_out):
    cases, count = z.shape[0], ones.shape[1]
    jump = mine[:cases, :count] - conds[:cases, :count]
    jump_out[...] = jump
    local[...] = sink[...] * z[...] + times_ones(mean_of(mine, conds, cases, count) * jump, ones[...], True)


def folded(value):
    total = value[:, :BR]
    for i in range(1, value.shape[1] // BR):
        total = total + value[:, i * BR : (i + 1) * BR]
    return total


def across_lanes(value):
    return jnp.sum(value, axis=1, keepdims=True)


def largest_of(blocks, pads):
    size = jnp.maximum(
        jnp.max(jnp.abs(blocks), axis=1, keepdims=True), jnp.max(jnp.abs(pads), axis=1, keepdims=True)
    )
    return jnp.where(size > 0.0, size, 1.0)


def case_row(columns):
    cases = columns[0].shape[0]
    total = jnp.where(lanes_of(cases, 0), columns[0], 0.0)
    for slot in range(1, len(columns)):
        total = jnp.where(lanes_of(cases, slot), columns[slot], total)
    return jnp.sum(total, axis=0, keepdims=True)


def shares_kernel(rhs, z, image, precond, sink, picked, product, jump, mine, conds, top, known, guide):
    cases, count = jump.shape
    start = z[...]
    bulk = 0.25 * (4.0 / top[0:1, 0:1])
    mean = mean_of(mine, conds, cases, count)
    size = largest_of(picked[...], jump[...])
    inverse = 1.0 / size
    unit = picked[...] * inverse
    unit_jump = jump[...] * inverse
    unit_own = start * inverse
    pulled = (product[...] * bulk) * inverse
    energy = across_lanes(folded(unit * pulled) + bulk * folded(sink[...] * unit_own * unit_own))
    energy = energy + 0.5 * bulk * across_lanes(mean * unit_jump * unit_jump)
    norm = across_lanes(folded(rhs[...] * start))
    curve = across_lanes(folded(start * image[...]))
    reach = jnp.max(jnp.abs(image[...]), axis=1, keepdims=True)
    still = reach <= 0.0
    scale = size / jnp.where(still, 1.0, reach)
    guess = jnp.where(curve > 0.0, norm / jnp.where(curve > 0.0, curve, 1.0), 0.0)
    guess = jnp.where(still, 1.0, jnp.clip(guess, scale * (1.0 / 1024.0), scale * 8.0))
    moved = guess * image[...]
    rest = rhs[...] - moved
    weighted = precond[...] * moved
    known[0:1] = case_row([norm, guess, across_lanes(folded(precond[...] * rest * rest)), across_lanes(folded(weighted * rest))])
    known[1:2] = case_row(
        [across_lanes(folded(weighted * moved)), size, energy, jnp.broadcast_to(top[0:1, 0:1], size.shape)]
    )
    tilt = jnp.where(norm > 0.0, curve / jnp.where(norm > 0.0, norm, 1.0), 0.0) * size
    guide[0] = jnp.broadcast_to(jnp.clip(tilt, -1e37, 1e37), guide.shape[1:])
    guide[1] = jnp.broadcast_to(inverse, guide.shape[1:])


def put_tiles(ref, start, block):
    tiles = block.shape[0] // 8
    ref[start * tiles : (start + 1) * tiles] = block.reshape(tiles, 8, BR)


def second_kernel(
    places, high, middle, low, p2, p1, own, a, b, there, conds, mine, ones, sink, top,
    start_picked, start_product, start_jump, start_own, known, guide,
    back, to_p1, to_p2, kept, sums,
):
    touched = high.shape[0] // BR
    cases = own.shape[1]
    count = ones.shape[1]
    less = 4.0 / top[0:1, 0:1]
    picked = picked_blocks(places, held_blocks(p2, p1, own, a, b), touched)
    product = product_of((picked * less) * (1.0 / 1024.0), high, middle, low)
    scales = jnp.concatenate([there[4, 0:1], there[4, 1:2]], axis=1)
    values = scales * wide(there[0:2] + b[4:6])
    pads = conds[cases + 8 : cases + 9, :count].astype(jnp.int32)
    here = wide(own)
    jump = times_ones(here, ones[...], False) - times_ones(values, pad_matrix(pads, values.shape[1]), False)
    mean = mean_of(mine, conds, cases, count)
    local = sink[...] * here + times_ones(mean * jump, ones[...], True)
    local = (local * less) * (1.0 / 4096.0)
    size = largest_of(picked, jump)
    inverse = 1.0 / size
    bulk = 0.25 * less
    tilt = jnp.clip(guide[0, :, 0:1] * inverse, -1e3, 1e3)
    unit = guide[1, :, 0:1]
    tilted = tilt * unit
    rest = picked * inverse - tilted * start_picked[...]
    pulled = product * (1024.0 * inverse) - (start_product[...] * bulk) * tilted
    rest_own = here * inverse - tilted * start_own[...]
    rest_jump = jump * inverse - tilted * start_jump[...]
    sunk = sink[...] * rest_own
    tied = 0.5 * mean * rest_jump
    tail = jnp.zeros((cases, BR - count), F32)
    energy = folded(rest * pulled) + bulk * folded(sunk * rest_own)
    energy = energy + bulk * jnp.concatenate([tied * rest_jump, tail], axis=1)
    cross = folded(start_picked[...] * unit * pulled) + bulk * folded(sunk * (start_own[...] * unit))
    cross = cross + bulk * jnp.concatenate([tied * (start_jump[...] * unit), tail], axis=1)
    own_row = case_row([size, tilt, across_lanes(cross), across_lanes(energy)])
    total = jnp.concatenate([known[0:2], own_row, jnp.zeros_like(own_row)])
    sums[...] = jnp.broadcast_to(total[None], sums.shape)
    landed = landed_blocks(places, product)
    for j in range(2):
        put_tiles(to_p2, j, landed[j])
    for j in range(4):
        put_tiles(back, j, landed[10 + j])
        put_tiles(to_p1, j, landed[2 + j])
    to_p2[to_p2.shape[0] - 1] = top[...]
    to_p1[to_p1.shape[0] - 1] = top[...]
    back[back.shape[0] - 1] = jnp.zeros_like(top)
    kept[0] = landed[6] + local[:, :BR]
    kept[1] = landed[7] + local[:, BR:]
    kept[2] = landed[8]
    kept[3] = landed[9]


def part_kernel(places, kept, local, from_p1, from_p2, precond, top, part):
    cases = kept.shape[1]
    near, far = [spot(places, places.shape[0] - 2 + i, cases)[None] for i in range(2)]
    one = from_p1[...] * near
    mine = kept[0:2] + one[0:2] + from_p2[...] * far
    part[0] = mine[0] + local[:, :BR]
    part[1] = mine[1] + local[:, BR:]
    part[2:4] = kept[2:4] + one[2:4]
    part[4] = jnp.zeros(part.shape[1:], F32)
    part[4, 0:1] = precond[:, :BR]
    part[4, 1:2] = precond[:, BR:]
    part[4, 8:16] = top[...]


def turn_kernel(part, there, precond, image_out, both_out, own_out, top_out):
    image = wide(part[0:2] + there[2:4])
    other = part[2:4] + there[0:2]
    image_out[...] = image
    scaled = precond[...] * image
    put_wide(both_out, 0, scaled)
    put_wide(own_out, 0, scaled)
    both_out[2] = there[4, 0:1] * other[0]
    both_out[3] = there[4, 1:2] * other[1]
    top_out[...] = jnp.maximum(part[4, 8:16], there[4, 8:16])


def last_part_kernel(places, kept, from_p1, from_p2, top, mine, other, top_out):
    cases = kept.shape[1]
    tiles = cases // 8
    near, far = [places[places.shape[0] - 2 + i] for i in range(2)]
    near_top = from_p1[from_p1.shape[0] - 1]
    far_top = from_p2[from_p2.shape[0] - 1]
    most = jnp.maximum(top[...], jnp.maximum(near * near_top, far * far_top))
    here, one, two = top[...] / most, near * (near_top / most), far * (far_top / most)
    for j in range(4):
        block = kept[j].reshape(tiles, 8, BR) * here + from_p1[j * tiles : (j + 1) * tiles] * one
        if j < 2:
            block = block + from_p2[j * tiles : (j + 1) * tiles] * two
            mine[j] = block.reshape(cases, BR)
        else:
            other[(j - 2) * tiles : (j - 1) * tiles] = block
    other[other.shape[0] - 1] = most
    top_out[...] = most


def steps_kernel(sums, steps):
    cases = steps.shape[1]
    rows = [sums[:, i, :] for i in range(3)]

    def value(i):
        row = rows[i // 4]
        return row if i % 4 == 0 else pltpu.roll(row, BR - (i % 4) * cases, 1)

    norm, guess, rest, mixed, moved, size, energy, top, other_size, tilt, cross, other_energy = [
        value(i) for i in range(12)
    ]

    def everyone(terms):
        return jnp.sum(terms, axis=0, keepdims=True)

    norm = everyone(norm)
    alpha = norm / everyone((size * size * energy) * top)
    shift = alpha / guess - 1.0
    fresh = everyone(rest + shift * (shift * moved - 2.0 * mixed))
    grown = 1.0 + fresh / norm
    two = alpha * other_size
    one = grown * size - two * tilt
    bend = everyone(((one * one) * energy + two * (two * other_energy - 2.0 * one * cross)) * top)
    for i, row in enumerate((alpha, grown, fresh / bend)):
        steps[i] = jnp.broadcast_to(as_column(row, 0, cases), steps.shape[1:])


def end_kernel(rhs, z, image, scaled, mine, mine_top, there, steps, solution, residual):
    cases = solution.shape[0]
    tiles = cases // 8
    alpha, grown, step = [wide([steps[i], steps[i]]) for i in range(3)]
    start = z[...]
    direction = grown * start - alpha * wide(scaled)
    solution[...] = alpha * start + step * direction
    there_top = there[there.shape[0] - 1]
    most = jnp.maximum(mine_top[...], there_top)
    here, away = spot([mine_top[...] / most], 0, cases), spot([there_top / most], 0, cases)
    blocks = [mine[j] * here + there[j * tiles : (j + 1) * tiles].reshape(cases, BR) * away for j in range(2)]
    bulk = spot([most], 0, cases)
    second = ((alpha * wide(blocks)) * wide([bulk, bulk])) * 1024.0
    residual[...] = rhs[...] - alpha * image[...] - step * (grown * image[...] - second)


def call(kernel, outs, *operands, scratch=(), far=(), grant=32):
    def space(outside, i):
        return pl.BlockSpec(memory_space=pl.ANY if i in outside else pltpu.VMEM)

    return pl.pallas_call(
        kernel,
        in_specs=[space(far, i) for i in range(len(operands))],
        out_specs=[space((), i) for i in range(len(outs))],
        out_shape=[jax.ShapeDtypeStruct(shape, kind) for shape, kind in outs],
        scratch_shapes=list(scratch),
        compiler_params=pltpu.CompilerParams(vmem_limit_bytes=grant * 1024 * 1024),
    )(*operands)


def on_device(rhs, schur, block_list, pad_rows, pad_cond, sink, precond):
    matrix = schur[0]
    cases, owned = rhs.shape[1:]
    inner = matrix.shape[0]
    blocks = owned // BR
    touched = inner // BR
    count = lax.axis_size("sub")
    everyone = count * lax.axis_size("board")
    pads = pad_rows.shape[1]
    swap = [(i, i ^ 1) for i in range(count)]
    across = [(i, i ^ 1) for i in range(lax.axis_size("board"))]
    near, far = climb(count, 1), leap(count)
    pair = ((blocks, cases, BR), F32)
    both = ((2 * blocks, cases, BR), F32)
    tile = ((8, BR), F32)
    full = ((cases, owned), F32)
    semaphores = pltpu.SemaphoreType.DMA

    z = barrier(precond * rhs[0])
    ones, pads_sent = call(begin_kernel, [((owned, pads), HALF), ((4 * cases + 8, BR), F32)], z, pad_rows, pad_cond)
    chunks = touched
    spots = 2 * (2 * REACH + 1)
    high, middle, low, places, top = call(
        prepare_kernel,
        [((inner, inner), HALF)] * 3 + [((touched * spots + 2, 8, BR), F32), tile],
        matrix, block_list,
        far=range(1),
        scratch=[pltpu.VMEM((inner, inner), F32), semaphores((chunks,))],
        grant=48,
    )

    def collect(back, to_p1, to_p2):
        from_p2 = lax.ppermute(to_p2, "sub", far)
        to_p1 = to_p1 + lax.ppermute(back, "sub", swap)
        return to_p1, from_p2

    other = lax.ppermute(z, "sub", swap)
    p2 = lax.ppermute(z, "sub", far)
    p1 = lax.ppermute(jnp.stack([z, other]), "sub", near)
    p1, p2, high, middle, low, places, top = barrier((p1, p2, high, middle, low, places, top))
    b = lax.ppermute(p1, "sub", swap)
    split = (places, high, middle, low)
    back, to_p1, to_p2, kept, start_picked, start_product = call(
        first_kernel,
        [both, both, pair, both, ((cases, inner), F32), ((cases, inner), F32)],
        *split, p2, p1, z, other, b,
    )
    conds = lax.ppermute(pads_sent, "board", across)
    local, start_jump = call(ties_kernel, [full, ((cases, pads), F32)], z, pads_sent, conds, ones, sink)
    to_p1, from_p2 = collect(back, to_p1, to_p2)
    from_p1 = lax.ppermute(to_p1, "sub", turned(near))
    (part,) = call(part_kernel, [((2 * blocks + 1, cases, BR), F32)], places, kept, local, from_p1, from_p2, precond, top)
    part_there = lax.ppermute(part, "sub", swap)
    part_across = lax.ppermute(part, "board", across)
    image, four, own, top = call(turn_kernel, [full, both, pair, tile], part, part_there, precond)
    known, guide = call(
        shares_kernel,
        [((2, BR), F32), ((2, cases, BR), F32)],
        rhs[0], z, image, precond, sink, start_picked, start_product, start_jump, pads_sent, conds, top,
    )
    p1 = lax.ppermute(four, "sub", near)
    p2 = lax.ppermute(own, "sub", far)
    p1, p2, part_across, known, guide = barrier((p1, p2, part_across, known, guide))
    b = lax.ppermute(jnp.concatenate([p1, part_across[blocks : 2 * blocks]]), "sub", swap)
    tiles = cases // 8
    back, to_p1, to_p2, kept, sums = call(
        second_kernel,
        [((4 * tiles + 1, 8, BR), F32)] * 2 + [((2 * tiles + 1, 8, BR), F32), both, ((everyone, 4, BR), F32)],
        *split, p2, p1, own, four[blocks:], b, part_across, conds, pads_sent, ones, sink, top,
        start_picked, start_product, start_jump, z, known, guide,
    )
    to_p1, from_p2 = collect(back, to_p1, to_p2)
    from_p1 = lax.ppermute(to_p1, "sub", turned(near))
    all_sums = lax.all_to_all(sums, ("board", "sub"), 0, 0)
    mine, to_other, mine_top = call(
        last_part_kernel, [pair, ((2 * tiles + 1, 8, BR), F32), tile], places, kept, from_p1, from_p2, top
    )
    there = lax.ppermute(to_other, "sub", swap)
    all_sums, there = barrier((all_sums, there))
    (steps,) = call(steps_kernel, [((3, cases, BR), F32)], all_sums)
    solution, residual = call(
        end_kernel, [full, full], rhs[0], z, image, own, mine, mine_top, there, steps
    )
    return (solution[None], residual[None])


def solution(mesh):
    in_specs = (
        P("board", None, "sub"),
        P("board", "sub", None),
        P("board", "sub"),
        P("board", "sub"),
        P("board", "sub"),
        P("board", "sub"),
        P("board", "sub"),
    )
    out_specs = (P("board", None, "sub"), P("board", None, "sub"))
    return jax.shard_map(
        on_device, mesh=mesh, in_specs=in_specs, out_specs=out_specs, check_vma=False
    )
```

```python
import jax
import jax.numpy as jnp
from jax import lax
from jax.experimental import pallas as pl
from jax.experimental.pallas import tpu as pltpu
from jax.sharding import PartitionSpec as P

BR = 128
REACH = 3
F32 = jnp.float32
HALF = jnp.bfloat16
barrier = lax.optimization_barrier


def climb(count, step):
    pairs = []
    for source in range(count):
        chip, core = divmod(source, 2)
        target = chip - step if core else chip + step
        inside = 0 <= target < count // 2
        pairs.append((source, target * 2 + core if inside else source ^ 1))
    return pairs


def leap(count):
    pairs = []
    for source in range(count):
        chip, core = divmod(source, 2)
        target = chip + 2 if core else chip - 2
        if 0 <= target < count // 2:
            pairs.append((source, target * 2 + 1 - core))
        else:
            pairs.append((source, source ^ 2))
    return pairs


def turned(pairs):
    return [(target, source) for source, target in pairs]


def thirds(value):
    high = value.astype(HALF)
    rest = value - high.astype(F32)
    middle = rest.astype(HALF)
    return high, middle, (rest - middle.astype(F32)).astype(HALF)


def dot(left, right):
    return jnp.dot(left, right, preferred_element_type=F32)


def times_ones(value, ones, turn):
    rows = value.shape[0]
    parts = jnp.concatenate(thirds(value))
    if turn:
        out = lax.dot_general(parts, ones, (((1,), (1,)), ((), ())), preferred_element_type=F32)
    else:
        out = dot(parts, ones)
    return out[:rows] + (out[rows : 2 * rows] + out[2 * rows :])


def pad_matrix(pad_rows, owned):
    here = lax.broadcasted_iota(jnp.int32, (owned, pad_rows.shape[1]), 0)
    return (here == pad_rows).astype(F32).astype(HALF)


def product_of(value, high, middle, low):
    rows = value.shape[0]
    one, two, three = thirds(value)
    first = dot(jnp.concatenate([one, two, three]), high[...])
    second = dot(jnp.concatenate([one, two]), middle[...])
    small = first[2 * rows :] + second[rows:] + dot(one, low[...])
    return (small + (first[rows : 2 * rows] + second[:rows])) + first[:rows]


def wide(pair):
    return jnp.concatenate([pair[0], pair[1]], axis=1)


def put_wide(ref, start, value):
    ref[start] = value[:, :BR]
    ref[start + 1] = value[:, BR:]


def lanes_of(cases, slot):
    lane = lax.broadcasted_iota(jnp.int32, (cases, BR), 1)
    return lane == lax.broadcasted_iota(jnp.int32, (cases, BR), 0) + slot * cases


def as_column(row, slot, cases):
    return jnp.sum(jnp.where(lanes_of(cases, slot), row, 0.0), axis=1, keepdims=True)


def begin_kernel(z, pad_rows, pad_cond, ones_out, pads_out):
    cases = z.shape[0]
    owned, count = ones_out.shape
    ones = pad_matrix(pad_rows[...], owned)
    ones_out[...] = ones
    pads_out[...] = jnp.zeros_like(pads_out)
    pads_out[:cases, :count] = times_ones(z[...], ones, False)
    pads_out[cases : cases + 1, :count] = pad_cond[...]
    pads_out[cases + 8 : cases + 9, :count] = pad_rows[...].astype(F32)


def places_kernel(blocks, places):
    position = lax.axis_index("sub")
    chip, core = position // 2, lax.rem(position, 2)
    above, below = lax.axis_size("sub") // 2 - 1 - chip, chip
    touched = blocks.shape[1]
    listed = blocks[...]
    offset = listed // 2 - position
    mirrored = jnp.where(core == 0, offset, -offset)
    place = jnp.where(mirrored == 2, 6, jnp.where(mirrored == 3, 5, mirrored + REACH))
    place = place * 2 + lax.rem(listed, 2)
    spots = 2 * (2 * REACH + 1)
    for i in range(touched):
        here = jnp.broadcast_to(place[:, i : i + 1], places.shape[1:])
        for j in range(spots):
            places[i * spots + j] = (here == j).astype(F32)
    near = jnp.where(core == 0, above, below) >= 1
    far = jnp.where(core == 0, below, above) >= 2
    for i, sender in enumerate((near, far)):
        places[touched * spots + i] = jnp.full(places.shape[1:], sender.astype(F32))


def split_kernel(schur, high, middle, low, top, held, sems):
    chunk = held.shape[0] // sems.shape[0]
    copies = []
    for i in range(sems.shape[0]):
        rows = slice(i * chunk, (i + 1) * chunk)
        copies.append(pltpu.make_async_copy(schur.at[rows], held.at[rows], sems.at[i]))
    for copy in copies:
        copy.start()
    largest = jnp.ones((1, chunk), F32)
    for i, copy in enumerate(copies):
        rows = slice(i * chunk, (i + 1) * chunk)
        copy.wait()
        high[rows], middle[rows], low[rows] = thirds(0.25 * held[rows])
        largest = jnp.maximum(largest, jnp.max(held[rows, rows], axis=0, keepdims=True))
    top[...] = jnp.broadcast_to(jnp.max(largest, axis=1, keepdims=True), top.shape)


def spot(places, i, cases):
    return jnp.concatenate([places[i]] * (cases // 8))


def picked_blocks(places, held, touched):
    cases, spots = held[0].shape[0], len(held)
    picked = []
    for i in range(touched):
        total = spot(places, i * spots, cases) * held[0]
        for j in range(1, spots):
            total = total + spot(places, i * spots + j, cases) * held[j]
        picked.append(total)
    return jnp.concatenate(picked, axis=1)


def landed_blocks(places, product):
    cases, touched = product.shape[0], product.shape[1] // BR
    spots = (places.shape[0] - 2) // touched
    landed = []
    for j in range(spots):
        total = spot(places, j, cases) * product[:, :BR]
        for i in range(1, touched):
            total = total + spot(places, i * spots + j, cases) * product[:, i * BR : (i + 1) * BR]
        landed.append(total)
    return landed


def halves(*values):
    return [value[:, start : start + BR] for value in values for start in (0, BR)]


def held_blocks(p2, p1, own, a, b):
    return [p2[0], p2[1], p1[0], p1[1], p1[2], p1[3], own[0], own[1], a[0], a[1], b[0], b[1], b[2], b[3]]


def mean_of(mine, conds, cases, count):
    return 0.5 * (mine[cases : cases + 1, :count] + conds[cases : cases + 1, :count])


def first_kernel(
    places, high, middle, low, p2, p1, four, b, back, to_p1, to_p2, kept, picked_out, product_out
):
    touched = high.shape[0] // BR
    picked = picked_blocks(places, halves(p2, p1[0], p1[1], four[0], four[1], b[0], b[1]), touched)
    product = product_of(4.0 * picked, high, middle, low)
    landed = landed_blocks(places, product)
    for j in range(2):
        to_p2[j] = landed[j]
    for j in range(4):
        back[j] = landed[10 + j]
        to_p1[j] = landed[2 + j]
    for j in range(4):
        kept[j] = landed[6 + j]
    picked_out[...] = picked
    product_out[...] = product


def ties_kernel(z, mine, conds, ones, sink, local, jump_out):
    cases, count = z.shape[0], ones.shape[1]
    jump = mine[:cases, :count] - conds[:cases, :count]
    jump_out[...] = jump
    local[...] = sink[...] * z[...] + times_ones(mean_of(mine, conds, cases, count) * jump, ones[...], True)


def folded(value):
    total = value[:, :BR]
    for i in range(1, value.shape[1] // BR):
        total = total + value[:, i * BR : (i + 1) * BR]
    return total


def across_lanes(value):
    return jnp.sum(value, axis=1, keepdims=True)


def largest_of(blocks, pads):
    size = jnp.maximum(
        jnp.max(jnp.abs(blocks), axis=1, keepdims=True), jnp.max(jnp.abs(pads), axis=1, keepdims=True)
    )
    return jnp.where(size > 0.0, size, 1.0)


def case_row(columns):
    cases = columns[0].shape[0]
    total = jnp.where(lanes_of(cases, 0), columns[0], 0.0)
    for slot in range(1, len(columns)):
        total = jnp.where(lanes_of(cases, slot), columns[slot], total)
    return jnp.sum(total, axis=0, keepdims=True)


def shares_kernel(rhs, z, image, precond, sink, picked, product, jump, mine, conds, top, known, guide):
    cases, count = jump.shape
    start = z[...]
    bulk = 0.25 * (4.0 / top[0:1, 0:1])
    mean = mean_of(mine, conds, cases, count)
    size = largest_of(picked[...], jump[...])
    inverse = 1.0 / size
    unit = picked[...] * inverse
    unit_jump = jump[...] * inverse
    unit_own = start * inverse
    pulled = (product[...] * bulk) * inverse
    energy = across_lanes(folded(unit * pulled) + bulk * folded(sink[...] * unit_own * unit_own))
    energy = energy + 0.5 * bulk * across_lanes(mean * unit_jump * unit_jump)
    norm = across_lanes(folded(rhs[...] * start))
    curve = across_lanes(folded(start * image[...]))
    reach = jnp.max(jnp.abs(image[...]), axis=1, keepdims=True)
    still = reach <= 0.0
    scale = size / jnp.where(still, 1.0, reach)
    guess = jnp.where(curve > 0.0, norm / jnp.where(curve > 0.0, curve, 1.0), 0.0)
    guess = jnp.where(still, 1.0, jnp.clip(guess, scale * (1.0 / 1024.0), scale * 8.0))
    moved = guess * image[...]
    rest = rhs[...] - moved
    weighted = precond[...] * moved
    known[0:1] = case_row([norm, guess, across_lanes(folded(precond[...] * rest * rest)), across_lanes(folded(weighted * rest))])
    known[1:2] = case_row(
        [across_lanes(folded(weighted * moved)), size, energy, jnp.broadcast_to(top[0:1, 0:1], size.shape)]
    )
    tilt = jnp.where(norm > 0.0, curve / jnp.where(norm > 0.0, norm, 1.0), 0.0) * size
    guide[0] = jnp.broadcast_to(jnp.clip(tilt, -1e37, 1e37), guide.shape[1:])
    guide[1] = jnp.broadcast_to(inverse, guide.shape[1:])


def put_tiles(ref, start, block):
    tiles = block.shape[0] // 8
    ref[start * tiles : (start + 1) * tiles] = block.reshape(tiles, 8, BR)


def second_kernel(
    places, high, middle, low, p2, p1, own, a, b, there, conds, mine, ones, sink, top,
    start_picked, start_product, start_jump, start_own, known, guide,
    back, to_p1, to_p2, kept, sums,
):
    touched = high.shape[0] // BR
    cases = own.shape[1]
    count = ones.shape[1]
    less = 4.0 / top[0:1, 0:1]
    picked = picked_blocks(places, held_blocks(p2, p1, own, a, b), touched)
    product = product_of((picked * less) * (1.0 / 1024.0), high, middle, low)
    scales = jnp.concatenate([there[4, 0:1], there[4, 1:2]], axis=1)
    values = scales * wide(there[0:2] + b[4:6])
    pads = conds[cases + 8 : cases + 9, :count].astype(jnp.int32)
    here = wide(own)
    jump = times_ones(here, ones[...], False) - times_ones(values, pad_matrix(pads, values.shape[1]), False)
    mean = mean_of(mine, conds, cases, count)
    local = sink[...] * here + times_ones(mean * jump, ones[...], True)
    local = (local * less) * (1.0 / 4096.0)
    size = largest_of(picked, jump)
    inverse = 1.0 / size
    bulk = 0.25 * less
    tilt = jnp.clip(guide[0, :, 0:1] * inverse, -1e3, 1e3)
    unit = guide[1, :, 0:1]
    tilted = tilt * unit
    rest = picked * inverse - tilted * start_picked[...]
    pulled = product * (1024.0 * inverse) - (start_product[...] * bulk) * tilted
    rest_own = here * inverse - tilted * start_own[...]
    rest_jump = jump * inverse - tilted * start_jump[...]
    sunk = sink[...] * rest_own
    tied = 0.5 * mean * rest_jump
    tail = jnp.zeros((cases, BR - count), F32)
    energy = folded(rest * pulled) + bulk * folded(sunk * rest_own)
    energy = energy + bulk * jnp.concatenate([tied * rest_jump, tail], axis=1)
    cross = folded(start_picked[...] * unit * pulled) + bulk * folded(sunk * (start_own[...] * unit))
    cross = cross + bulk * jnp.concatenate([tied * (start_jump[...] * unit), tail], axis=1)
    own_row = case_row([size, tilt, across_lanes(cross), across_lanes(energy)])
    total = jnp.concatenate([known[0:2], own_row, jnp.zeros_like(own_row)])
    sums[...] = jnp.broadcast_to(total[None], sums.shape)
    landed = landed_blocks(places, product)
    for j in range(2):
        put_tiles(to_p2, j, landed[j])
    for j in range(4):
        put_tiles(back, j, landed[10 + j])
        put_tiles(to_p1, j, landed[2 + j])
    to_p2[to_p2.shape[0] - 1] = top[...]
    to_p1[to_p1.shape[0] - 1] = top[...]
    back[back.shape[0] - 1] = jnp.zeros_like(top)
    kept[0] = landed[6] + local[:, :BR]
    kept[1] = landed[7] + local[:, BR:]
    kept[2] = landed[8]
    kept[3] = landed[9]


def part_kernel(places, kept, local, from_p1, from_p2, precond, top, part):
    cases = kept.shape[1]
    near, far = [spot(places, places.shape[0] - 2 + i, cases)[None] for i in range(2)]
    one = from_p1[...] * near
    mine = kept[0:2] + one[0:2] + from_p2[...] * far
    part[0] = mine[0] + local[:, :BR]
    part[1] = mine[1] + local[:, BR:]
    part[2:4] = kept[2:4] + one[2:4]
    part[4] = jnp.zeros(part.shape[1:], F32)
    part[4, 0:1] = precond[:, :BR]
    part[4, 1:2] = precond[:, BR:]
    part[4, 8:16] = top[...]


def turn_kernel(part, there, precond, image_out, both_out, own_out, top_out):
    image = wide(part[0:2] + there[2:4])
    other = part[2:4] + there[0:2]
    image_out[...] = image
    scaled = precond[...] * image
    put_wide(both_out, 0, scaled)
    put_wide(own_out, 0, scaled)
    both_out[2] = there[4, 0:1] * other[0]
    both_out[3] = there[4, 1:2] * other[1]
    top_out[...] = jnp.maximum(part[4, 8:16], there[4, 8:16])


def last_part_kernel(places, kept, from_p1, from_p2, top, mine, other, top_out):
    cases = kept.shape[1]
    tiles = cases // 8
    near, far = [places[places.shape[0] - 2 + i] for i in range(2)]
    near_top = from_p1[from_p1.shape[0] - 1]
    far_top = from_p2[from_p2.shape[0] - 1]
    most = jnp.maximum(top[...], jnp.maximum(near * near_top, far * far_top))
    here, one, two = top[...] / most, near * (near_top / most), far * (far_top / most)
    for j in range(4):
        block = kept[j].reshape(tiles, 8, BR) * here + from_p1[j * tiles : (j + 1) * tiles] * one
        if j < 2:
            block = block + from_p2[j * tiles : (j + 1) * tiles] * two
            mine[j] = block.reshape(cases, BR)
        else:
            other[(j - 2) * tiles : (j - 1) * tiles] = block
    other[other.shape[0] - 1] = most
    top_out[...] = most


def steps_kernel(sums, steps):
    cases = steps.shape[1]
    rows = [sums[:, i, :] for i in range(3)]

    def value(i):
        row = rows[i // 4]
        return row if i % 4 == 0 else pltpu.roll(row, BR - (i % 4) * cases, 1)

    norm, guess, rest, mixed, moved, size, energy, top, other_size, tilt, cross, other_energy = [
        value(i) for i in range(12)
    ]

    def everyone(terms):
        return jnp.sum(terms, axis=0, keepdims=True)

    norm = everyone(norm)
    alpha = norm / everyone((size * size * energy) * top)
    shift = alpha / guess - 1.0
    fresh = everyone(rest + shift * (shift * moved - 2.0 * mixed))
    grown = 1.0 + fresh / norm
    two = alpha * other_size
    one = grown * size - two * tilt
    bend = everyone(((one * one) * energy + two * (two * other_energy - 2.0 * one * cross)) * top)
    for i, row in enumerate((alpha, grown, fresh / bend)):
        steps[i] = jnp.broadcast_to(as_column(row, 0, cases), steps.shape[1:])


def end_kernel(rhs, z, image, scaled, mine, mine_top, there, steps, solution, residual):
    cases = solution.shape[0]
    tiles = cases // 8
    alpha, grown, step = [wide([steps[i], steps[i]]) for i in range(3)]
    start = z[...]
    direction = grown * start - alpha * wide(scaled)
    solution[...] = alpha * start + step * direction
    there_top = there[there.shape[0] - 1]
    most = jnp.maximum(mine_top[...], there_top)
    here, away = spot([mine_top[...] / most], 0, cases), spot([there_top / most], 0, cases)
    blocks = [mine[j] * here + there[j * tiles : (j + 1) * tiles].reshape(cases, BR) * away for j in range(2)]
    bulk = spot([most], 0, cases)
    second = ((alpha * wide(blocks)) * wide([bulk, bulk])) * 1024.0
    residual[...] = rhs[...] - alpha * image[...] - step * (grown * image[...] - second)


def call(kernel, outs, *operands, scratch=(), far=(), grant=32):
    def space(outside, i):
        return pl.BlockSpec(memory_space=pl.ANY if i in outside else pltpu.VMEM)

    return pl.pallas_call(
        kernel,
        in_specs=[space(far, i) for i in range(len(operands))],
        out_specs=[space((), i) for i in range(len(outs))],
        out_shape=[jax.ShapeDtypeStruct(shape, kind) for shape, kind in outs],
        scratch_shapes=list(scratch),
        compiler_params=pltpu.CompilerParams(vmem_limit_bytes=grant * 1024 * 1024),
    )(*operands)


def on_device(rhs, schur, block_list, pad_rows, pad_cond, sink, precond):
    matrix = schur[0]
    cases, owned = rhs.shape[1:]
    inner = matrix.shape[0]
    blocks = owned // BR
    touched = inner // BR
    count = lax.axis_size("sub")
    everyone = count * lax.axis_size("board")
    pads = pad_rows.shape[1]
    swap = [(i, i ^ 1) for i in range(count)]
    across = [(i, i ^ 1) for i in range(lax.axis_size("board"))]
    near, far = climb(count, 1), leap(count)
    pair = ((blocks, cases, BR), F32)
    both = ((2 * blocks, cases, BR), F32)
    tile = ((8, BR), F32)
    full = ((cases, owned), F32)
    semaphores = pltpu.SemaphoreType.DMA

    z = barrier(precond * rhs[0])
    ones, pads_sent = call(begin_kernel, [((owned, pads), HALF), ((4 * cases + 8, BR), F32)], z, pad_rows, pad_cond)
    chunks = touched
    spots = 2 * (2 * REACH + 1)
    (places,) = call(places_kernel, [((touched * spots + 2, 8, BR), F32)], block_list)
    high, middle, low, top = call(
        split_kernel,
        [((inner, inner), HALF)] * 3 + [tile],
        matrix,
        far=range(1),
        scratch=[pltpu.VMEM((inner, inner), F32), semaphores((chunks,))],
        grant=49,
    )

    def collect(back, to_p1, to_p2):
        from_p2 = lax.ppermute(to_p2, "sub", far)
        to_p1 = to_p1 + lax.ppermute(back, "sub", swap)
        return to_p1, from_p2

    scale_there = lax.ppermute(precond, "sub", swap)
    four = barrier(jnp.stack([z, scale_there * lax.ppermute(rhs[0], "sub", swap)]))
    p2 = lax.ppermute(z, "sub", far)
    p1 = lax.ppermute(four, "sub", near)
    p1, p2, high, middle, low, top = barrier((p1, p2, high, middle, low, top))
    b = lax.ppermute(p1, "sub", swap)
    split = (places, high, middle, low)
    back, to_p1, to_p2, kept, start_picked, start_product = call(
        first_kernel,
        [both, both, pair, both, ((cases, inner), F32), ((cases, inner), F32)],
        *split, p2, p1, four, b,
    )
    conds = lax.ppermute(pads_sent, "board", across)
    local, start_jump = call(ties_kernel, [full, ((cases, pads), F32)], z, pads_sent, conds, ones, sink)
    to_p1, from_p2 = collect(back, to_p1, to_p2)
    from_p1 = lax.ppermute(to_p1, "sub", turned(near))
    (part,) = call(part_kernel, [((2 * blocks + 1, cases, BR), F32)], places, kept, local, from_p1, from_p2, precond, top)
    part_there = lax.ppermute(part, "sub", swap)
    part_across = lax.ppermute(part, "board", across)
    image, four, own, top = call(turn_kernel, [full, both, pair, tile], part, part_there, precond)
    known, guide = call(
        shares_kernel,
        [((2, BR), F32), ((2, cases, BR), F32)],
        rhs[0], z, image, precond, sink, start_picked, start_product, start_jump, pads_sent, conds, top,
    )
    p1 = lax.ppermute(four, "sub", near)
    p2 = lax.ppermute(own, "sub", far)
    p1, p2, part_across, known, guide = barrier((p1, p2, part_across, known, guide))
    b = lax.ppermute(jnp.concatenate([p1, part_across[blocks : 2 * blocks]]), "sub", swap)
    tiles = cases // 8
    back, to_p1, to_p2, kept, sums = call(
        second_kernel,
        [((4 * tiles + 1, 8, BR), F32)] * 2 + [((2 * tiles + 1, 8, BR), F32), both, ((everyone, 4, BR), F32)],
        *split, p2, p1, own, four[blocks:], b, part_across, conds, pads_sent, ones, sink, top,
        start_picked, start_product, start_jump, z, known, guide,
    )
    to_p1, from_p2 = collect(back, to_p1, to_p2)
    from_p1 = lax.ppermute(to_p1, "sub", turned(near))
    all_sums = lax.all_to_all(sums, ("board", "sub"), 0, 0)
    mine, to_other, mine_top = call(
        last_part_kernel, [pair, ((2 * tiles + 1, 8, BR), F32), tile], places, kept, from_p1, from_p2, top
    )
    there = lax.ppermute(to_other, "sub", swap)
    all_sums, there = barrier((all_sums, there))
    (steps,) = call(steps_kernel, [((3, cases, BR), F32)], all_sums)
    solution, residual = call(
        end_kernel, [full, full], rhs[0], z, image, own, mine, mine_top, there, steps
    )
    return (solution[None], residual[None])


def solution(mesh):
    in_specs = (
        P("board", None, "sub"),
        P("board", "sub", None),
        P("board", "sub"),
        P("board", "sub"),
        P("board", "sub"),
        P("board", "sub"),
        P("board", "sub"),
    )
    out_specs = (P("board", None, "sub"), P("board", None, "sub"))
    return jax.shard_map(
        on_device, mesh=mesh, in_specs=in_specs, out_specs=out_specs, check_vma=False
    )
```

```python
import jax
import jax.numpy as jnp
from jax import lax
from jax.experimental import pallas as pl
from jax.experimental.pallas import tpu as pltpu
from jax.sharding import PartitionSpec as P

BR = 128
REACH = 3
F32 = jnp.float32
HALF = jnp.bfloat16
barrier = lax.optimization_barrier


def climb(count, step):
    pairs = []
    for source in range(count):
        chip, core = divmod(source, 2)
        target = chip - step if core else chip + step
        inside = 0 <= target < count // 2
        pairs.append((source, target * 2 + core if inside else source ^ 1))
    return pairs


def leap(count):
    pairs = []
    for source in range(count):
        chip, core = divmod(source, 2)
        target = chip + 2 if core else chip - 2
        if 0 <= target < count // 2:
            pairs.append((source, target * 2 + 1 - core))
        else:
            pairs.append((source, source ^ 2))
    return pairs


def beside(count):
    pairs = []
    for source in range(count):
        chip, core = divmod(source, 2)
        target = chip + 1 if chip % 2 else chip - 1
        inside = 0 <= target < count // 2
        pairs.append((source, target * 2 + core if inside else source ^ 1))
    return pairs


def turned(pairs):
    return [(target, source) for source, target in pairs]


def thirds(value):
    high = value.astype(HALF)
    rest = value - high.astype(F32)
    middle = rest.astype(HALF)
    return high, middle, (rest - middle.astype(F32)).astype(HALF)


def dot(left, right):
    return jnp.dot(left, right, preferred_element_type=F32)


def times_ones(value, ones, turn):
    rows = value.shape[0]
    parts = jnp.concatenate(thirds(value))
    if turn:
        out = lax.dot_general(parts, ones, (((1,), (1,)), ((), ())), preferred_element_type=F32)
    else:
        out = dot(parts, ones)
    return out[:rows] + (out[rows : 2 * rows] + out[2 * rows :])


def pad_matrix(pad_rows, owned):
    here = lax.broadcasted_iota(jnp.int32, (owned, pad_rows.shape[1]), 0)
    return (here == pad_rows).astype(F32).astype(HALF)


def product_of(value, high, middle, low):
    rows = value.shape[0]
    one, two, three = thirds(value)
    first = dot(jnp.concatenate([one, two, three]), high[...])
    second = dot(jnp.concatenate([one, two]), middle[...])
    small = first[2 * rows :] + second[rows:] + dot(one, low[...])
    return (small + (first[rows : 2 * rows] + second[:rows])) + first[:rows]


def wide(pair):
    return jnp.concatenate([pair[0], pair[1]], axis=1)


def put_wide(ref, start, value):
    ref[start] = value[:, :BR]
    ref[start + 1] = value[:, BR:]


def lanes_of(cases, slot):
    lane = lax.broadcasted_iota(jnp.int32, (cases, BR), 1)
    return lane == lax.broadcasted_iota(jnp.int32, (cases, BR), 0) + slot * cases


def as_column(row, slot, cases):
    return jnp.sum(jnp.where(lanes_of(cases, slot), row, 0.0), axis=1, keepdims=True)


def begin_kernel(z, pad_rows, pad_cond, ones_out, pads_out):
    cases = z.shape[0]
    owned, count = ones_out.shape
    ones = pad_matrix(pad_rows[...], owned)
    ones_out[...] = ones
    pads_out[...] = jnp.zeros_like(pads_out)
    pads_out[:cases, :count] = times_ones(z[...], ones, False)
    pads_out[cases : cases + 1, :count] = pad_cond[...]
    pads_out[cases + 8 : cases + 9, :count] = pad_rows[...].astype(F32)


def places_kernel(blocks, places):
    position = lax.axis_index("sub")
    chip, core = position // 2, lax.rem(position, 2)
    above, below = lax.axis_size("sub") // 2 - 1 - chip, chip
    touched = blocks.shape[1]
    listed = blocks[...]
    offset = listed // 2 - position
    mirrored = jnp.where(core == 0, offset, -offset)
    place = jnp.where(mirrored == 2, 6, jnp.where(mirrored == 3, 5, mirrored + REACH))
    place = place * 2 + lax.rem(listed, 2)
    spots = 2 * (2 * REACH + 1)
    for i in range(touched):
        here = jnp.broadcast_to(place[:, i : i + 1], places.shape[1:])
        for j in range(spots):
            places[i * spots + j] = (here == j).astype(F32)
    near = jnp.where(core == 0, above, below) >= 1
    far = jnp.where(core == 0, below, above) >= 2
    odd = lax.rem(chip, 2) == 1
    cross = jnp.where(odd, above, below) >= 1
    inner = odd == (core == 0)
    for i, sender in enumerate((near, far, cross, inner)):
        places[touched * spots + i] = jnp.full(places.shape[1:], sender.astype(F32))


def split_kernel(schur, high, middle, low, top, held, sems):
    chunk = held.shape[0] // sems.shape[0]
    copies = []
    for i in range(sems.shape[0]):
        rows = slice(i * chunk, (i + 1) * chunk)
        copies.append(pltpu.make_async_copy(schur.at[rows], held.at[rows], sems.at[i]))
    for copy in copies:
        copy.start()
    largest = jnp.ones((1, chunk), F32)
    for i, copy in enumerate(copies):
        rows = slice(i * chunk, (i + 1) * chunk)
        copy.wait()
        high[rows], middle[rows], low[rows] = thirds(0.25 * held[rows])
        largest = jnp.maximum(largest, jnp.max(held[rows, rows], axis=0, keepdims=True))
    top[...] = jnp.broadcast_to(jnp.max(largest, axis=1, keepdims=True), top.shape)


def spot(places, i, cases):
    return jnp.concatenate([places[i]] * (cases // 8))


def picked_blocks(places, held, touched):
    cases, spots = held[0].shape[0], len(held)
    picked = []
    for i in range(touched):
        total = spot(places, i * spots, cases) * held[0]
        for j in range(1, spots):
            total = total + spot(places, i * spots + j, cases) * held[j]
        picked.append(total)
    return jnp.concatenate(picked, axis=1)


def landed_blocks(places, product):
    cases, touched = product.shape[0], product.shape[1] // BR
    spots = (places.shape[0] - 4) // touched
    landed = []
    for j in range(spots):
        total = spot(places, j, cases) * product[:, :BR]
        for i in range(1, touched):
            total = total + spot(places, i * spots + j, cases) * product[:, i * BR : (i + 1) * BR]
        landed.append(total)
    return landed


def halves(*values):
    return [value[:, start : start + BR] for value in values for start in (0, BR)]


def held_blocks(p2, p1, own, a, b):
    return [p2[0], p2[1], p1[0], p1[1], p1[2], p1[3], own[0], own[1], a[0], a[1], b[0], b[1], b[2], b[3]]


def mean_of(mine, conds, cases, count):
    return 0.5 * (mine[cases : cases + 1, :count] + conds[cases : cases + 1, :count])


def first_kernel(
    places, high, middle, low, p2, p1, four, b, back, to_p1, to_p2, kept, picked_out, product_out
):
    touched = high.shape[0] // BR
    picked = picked_blocks(places, halves(p2, p1[0], p1[1], four[0], four[1], b[0], b[1]), touched)
    product = product_of(4.0 * picked, high, middle, low)
    landed = landed_blocks(places, product)
    for j in range(2):
        to_p2[j] = landed[j]
    for j in range(4):
        back[j] = landed[10 + j]
        to_p1[j] = landed[2 + j]
    for j in range(4):
        kept[j] = landed[6 + j]
    picked_out[...] = picked
    product_out[...] = product


def ties_kernel(z, mine, conds, ones, sink, local, jump_out, ones_there):
    cases, count = z.shape[0], ones.shape[1]
    jump = mine[:cases, :count] - conds[:cases, :count]
    jump_out[...] = jump
    pads = conds[cases + 8 : cases + 9, :count].astype(jnp.int32)
    ones_there[...] = pad_matrix(pads, z.shape[1])
    local[...] = sink[...] * z[...] + times_ones(mean_of(mine, conds, cases, count) * jump, ones[...], True)


def folded(value):
    total = value[:, :BR]
    for i in range(1, value.shape[1] // BR):
        total = total + value[:, i * BR : (i + 1) * BR]
    return total


def across_lanes(value):
    return jnp.sum(value, axis=1, keepdims=True)


def largest_of(blocks, pads):
    size = jnp.maximum(
        jnp.max(jnp.abs(blocks), axis=1, keepdims=True), jnp.max(jnp.abs(pads), axis=1, keepdims=True)
    )
    return jnp.where(size > 0.0, size, 1.0)


def case_row(columns):
    cases = columns[0].shape[0]
    total = jnp.where(lanes_of(cases, 0), columns[0], 0.0)
    for slot in range(1, len(columns)):
        total = jnp.where(lanes_of(cases, slot), columns[slot], total)
    return jnp.sum(total, axis=0, keepdims=True)


def shares_kernel(
    rhs, z, image, scaled, ones, precond, sink, picked, product, jump, mine, conds, top, known, guide, at_pads
):
    cases, count = jump.shape
    at_pads[...] = times_ones(wide(scaled), ones[...], False)
    start = z[...]
    bulk = 0.25 * (4.0 / top[0:1, 0:1])
    mean = mean_of(mine, conds, cases, count)
    size = largest_of(picked[...], jump[...])
    inverse = 1.0 / size
    unit = picked[...] * inverse
    unit_jump = jump[...] * inverse
    unit_own = start * inverse
    pulled = (product[...] * bulk) * inverse
    energy = across_lanes(folded(unit * pulled) + bulk * folded(sink[...] * unit_own * unit_own))
    energy = energy + 0.5 * bulk * across_lanes(mean * unit_jump * unit_jump)
    norm = across_lanes(folded(rhs[...] * start))
    curve = across_lanes(folded(start * image[...]))
    reach = jnp.max(jnp.abs(image[...]), axis=1, keepdims=True)
    still = reach <= 0.0
    scale = size / jnp.where(still, 1.0, reach)
    guess = jnp.where(curve > 0.0, norm / jnp.where(curve > 0.0, curve, 1.0), 0.0)
    guess = jnp.where(still, 1.0, jnp.clip(guess, scale * (1.0 / 1024.0), scale * 8.0))
    moved = guess * image[...]
    rest = rhs[...] - moved
    weighted = precond[...] * moved
    known[0:1] = case_row([norm, guess, across_lanes(folded(precond[...] * rest * rest)), across_lanes(folded(weighted * rest))])
    known[1:2] = case_row(
        [across_lanes(folded(weighted * moved)), size, energy, jnp.broadcast_to(top[0:1, 0:1], size.shape)]
    )
    tilt = jnp.where(norm > 0.0, curve / jnp.where(norm > 0.0, norm, 1.0), 0.0) * size
    guide[0] = jnp.broadcast_to(jnp.clip(tilt, -1e37, 1e37), guide.shape[1:])
    guide[1] = jnp.broadcast_to(inverse, guide.shape[1:])


def put_tiles(ref, start, block):
    tiles = block.shape[0] // 8
    ref[start * tiles : (start + 1) * tiles] = block.reshape(tiles, 8, BR)


def second_kernel(
    places, high, middle, low, p2, p1, own, a, b, there, conds, mine, ones, ones_there, at_pads, sink, top,
    start_picked, start_product, start_jump, start_own, known, guide,
    given, stays, to_p2, sums,
):
    touched = high.shape[0] // BR
    cases = own.shape[1]
    count = ones.shape[1]
    less = 4.0 / top[0:1, 0:1]
    picked = picked_blocks(places, held_blocks(p2, p1, own, a, b), touched)
    product = product_of((picked * less) * (1.0 / 1024.0), high, middle, low)
    here = wide(own)
    jump = at_pads[...] - times_ones(wide(there[0:2]), ones_there[...], False)
    mean = mean_of(mine, conds, cases, count)
    local = sink[...] * here + times_ones(mean * jump, ones[...], True)
    local = (local * less) * (1.0 / 4096.0)
    size = largest_of(picked, jump)
    inverse = 1.0 / size
    bulk = 0.25 * less
    tilt = jnp.clip(guide[0, :, 0:1] * inverse, -1e3, 1e3)
    unit = guide[1, :, 0:1]
    tilted = tilt * unit
    rest = picked * inverse - tilted * start_picked[...]
    pulled = product * (1024.0 * inverse) - (start_product[...] * bulk) * tilted
    rest_own = here * inverse - tilted * start_own[...]
    rest_jump = jump * inverse - tilted * start_jump[...]
    sunk = sink[...] * rest_own
    tied = 0.5 * mean * rest_jump
    tail = jnp.zeros((cases, BR - count), F32)
    energy = folded(rest * pulled) + bulk * folded(sunk * rest_own)
    energy = energy + bulk * jnp.concatenate([tied * rest_jump, tail], axis=1)
    cross = folded(start_picked[...] * unit * pulled) + bulk * folded(sunk * (start_own[...] * unit))
    cross = cross + bulk * jnp.concatenate([tied * (start_jump[...] * unit), tail], axis=1)
    own_row = case_row([size, tilt, across_lanes(cross), across_lanes(energy)])
    total = jnp.concatenate([known[0:2], own_row, jnp.zeros_like(own_row)])
    sums[...] = jnp.broadcast_to(total[None], sums.shape)
    landed = landed_blocks(places, product)
    for j in range(2):
        put_tiles(to_p2, j, landed[j])
        put_tiles(given, j, landed[4 + j])
        put_tiles(given, 2 + j, landed[10 + j])
        put_tiles(given, 4 + j, landed[8 + j])
        put_tiles(stays, j, landed[2 + j])
        put_tiles(stays, 2 + j, landed[12 + j])
        put_tiles(stays, 4 + j, landed[6 + j] + local[:, j * BR : (j + 1) * BR])
    to_p2[to_p2.shape[0] - 1] = top[...]


def part_kernel(places, kept, local, from_p1, from_p2, precond, top, part):
    cases = kept.shape[1]
    near, far = [spot(places, places.shape[0] - 4 + i, cases)[None] for i in range(2)]
    one = from_p1[...] * near
    mine = kept[0:2] + one[0:2] + from_p2[...] * far
    part[0] = mine[0] + local[:, :BR]
    part[1] = mine[1] + local[:, BR:]
    part[2:4] = kept[2:4] + one[2:4]
    part[4] = jnp.zeros(part.shape[1:], F32)
    part[4, 0:1] = precond[:, :BR]
    part[4, 1:2] = precond[:, BR:]
    part[4, 8:16] = top[...]


def turn_kernel(part, there, precond, image_out, both_out, own_out, top_out):
    image = wide(part[0:2] + there[2:4])
    other = part[2:4] + there[0:2]
    image_out[...] = image
    scaled = precond[...] * image
    put_wide(both_out, 0, scaled)
    put_wide(own_out, 0, scaled)
    both_out[2] = there[4, 0:1] * other[0]
    both_out[3] = there[4, 1:2] * other[1]
    top_out[...] = jnp.maximum(part[4, 8:16], there[4, 8:16])


def sort_kernel(places, given, stays, top, to_e, to_o, own):
    pair = stays.shape[0] // 3
    inner = places[places.shape[0] - 1] > 0.0
    for i in range(pair):
        near = stays[i] + given[pair + i]
        away = stays[pair + i] + given[i]
        to_e[i] = jnp.where(inner, near, away)
        to_o[i] = jnp.where(inner, away, near)
        own[i] = stays[2 * pair + i] + given[2 * pair + i]
    to_e[pair] = top[...]
    to_o[pair] = top[...]


def steps_kernel(sums, steps):
    cases = steps.shape[1]
    rows = [sums[:, i, :] for i in range(3)]

    def value(i):
        row = rows[i // 4]
        return row if i % 4 == 0 else pltpu.roll(row, BR - (i % 4) * cases, 1)

    norm, guess, rest, mixed, moved, size, energy, top, other_size, tilt, cross, other_energy = [
        value(i) for i in range(12)
    ]

    def everyone(terms):
        return jnp.sum(terms, axis=0, keepdims=True)

    norm = everyone(norm)
    alpha = norm / everyone((size * size * energy) * top)
    shift = alpha / guess - 1.0
    fresh = everyone(rest + shift * (shift * moved - 2.0 * mixed))
    grown = 1.0 + fresh / norm
    two = alpha * other_size
    one = grown * size - two * tilt
    bend = everyone(((one * one) * energy + two * (two * other_energy - 2.0 * one * cross)) * top)
    for i, row in enumerate((alpha, grown, fresh / bend)):
        steps[i] = jnp.broadcast_to(as_column(row, 0, cases), steps.shape[1:])


def end_kernel(rhs, z, image, scaled, places, own, from_e, from_o, from_p2, top, steps, solution, residual):
    cases = solution.shape[0]
    tiles = cases // 8
    alpha, grown, step = [wide([steps[i], steps[i]]) for i in range(3)]
    start = z[...]
    direction = grown * start - alpha * wide(scaled)
    solution[...] = alpha * start + step * direction
    one = jnp.ones_like(top)
    cross, far = places[places.shape[0] - 2], places[places.shape[0] - 3]
    parts = [(own, top[...], one)] + [
        (part, part[2 * tiles], valid) for part, valid in ((from_e, one), (from_o, cross), (from_p2, far))
    ]
    most = top[...]
    for _, scale, valid in parts[1:]:
        most = jnp.maximum(most, valid * scale)
    total = 0.0
    for part, scale, valid in parts:
        factor = valid * (scale / most)
        total = total + part[: 2 * tiles] * factor[None]
    blocks = total.reshape(2, cases, BR)
    bulk = spot([most], 0, cases)
    second = ((alpha * wide(blocks)) * wide([bulk, bulk])) * 1024.0
    residual[...] = rhs[...] - alpha * image[...] - step * (grown * image[...] - second)


def call(kernel, outs, *operands, scratch=(), far=(), grant=32):
    def space(outside, i):
        return pl.BlockSpec(memory_space=pl.ANY if i in outside else pltpu.VMEM)

    return pl.pallas_call(
        kernel,
        in_specs=[space(far, i) for i in range(len(operands))],
        out_specs=[space((), i) for i in range(len(outs))],
        out_shape=[jax.ShapeDtypeStruct(shape, kind) for shape, kind in outs],
        scratch_shapes=list(scratch),
        compiler_params=pltpu.CompilerParams(vmem_limit_bytes=grant * 1024 * 1024),
    )(*operands)


def on_device(rhs, schur, block_list, pad_rows, pad_cond, sink, precond):
    matrix = schur[0]
    cases, owned = rhs.shape[1:]
    inner = matrix.shape[0]
    blocks = owned // BR
    touched = inner // BR
    count = lax.axis_size("sub")
    everyone = count * lax.axis_size("board")
    pads = pad_rows.shape[1]
    swap = [(i, i ^ 1) for i in range(count)]
    across = [(i, i ^ 1) for i in range(lax.axis_size("board"))]
    near, far = climb(count, 1), leap(count)
    pair = ((blocks, cases, BR), F32)
    both = ((2 * blocks, cases, BR), F32)
    tile = ((8, BR), F32)
    full = ((cases, owned), F32)
    semaphores = pltpu.SemaphoreType.DMA

    z = barrier(precond * rhs[0])
    ones, pads_sent = call(begin_kernel, [((owned, pads), HALF), ((4 * cases + 8, BR), F32)], z, pad_rows, pad_cond)
    chunks = touched
    spots = 2 * (2 * REACH + 1)
    (places,) = call(places_kernel, [((touched * spots + 4, 8, BR), F32)], block_list)
    high, middle, low, top = call(
        split_kernel,
        [((inner, inner), HALF)] * 3 + [tile],
        matrix,
        far=range(1),
        scratch=[pltpu.VMEM((inner, inner), F32), semaphores((chunks,))],
        grant=49,
    )

    def collect(back, to_p1, to_p2):
        from_p2 = lax.ppermute(to_p2, "sub", far)
        to_p1 = to_p1 + lax.ppermute(back, "sub", swap)
        return to_p1, from_p2

    scale_there = lax.ppermute(precond, "sub", swap)
    four = barrier(jnp.stack([z, scale_there * lax.ppermute(rhs[0], "sub", swap)]))
    p2 = lax.ppermute(z, "sub", far)
    p1 = lax.ppermute(four, "sub", near)
    p1, p2, high, middle, low, top = barrier((p1, p2, high, middle, low, top))
    b = lax.ppermute(p1, "sub", swap)
    b, ones, pads_sent = barrier((b, ones, pads_sent))
    split = (places, high, middle, low)
    back, to_p1, to_p2, kept, start_picked, start_product = call(
        first_kernel,
        [both, both, pair, both, ((cases, inner), F32), ((cases, inner), F32)],
        *split, p2, p1, four, b,
    )
    conds = lax.ppermute(pads_sent, "board", across)
    local, start_jump, ones_there = call(
        ties_kernel,
        [full, ((cases, pads), F32), ((owned, pads), HALF)],
        z, pads_sent, conds, ones, sink,
    )
    to_p1, from_p2 = collect(back, to_p1, to_p2)
    from_p1 = lax.ppermute(to_p1, "sub", turned(near))
    (part,) = call(part_kernel, [((2 * blocks + 1, cases, BR), F32)], places, kept, local, from_p1, from_p2, precond, top)
    part_there = lax.ppermute(part, "sub", swap)
    image, four, own, top = call(turn_kernel, [full, both, pair, tile], part, part_there, precond)
    known, guide, at_pads = call(
        shares_kernel,
        [((2, BR), F32), ((2, cases, BR), F32), ((cases, pads), F32)],
        rhs[0], z, image, own, ones, precond, sink, start_picked, start_product, start_jump, pads_sent, conds, top,
    )
    p1 = lax.ppermute(four, "sub", near)
    p2 = lax.ppermute(own, "sub", far)
    there = lax.ppermute(four, "board", across)
    p1, p2, known, guide, at_pads = barrier((p1, p2, known, guide, at_pads))
    b = lax.ppermute(p1, "sub", swap)
    tiles = cases // 8
    pair_tiles = ((2 * tiles, 8, BR), F32)
    sent = ((2 * tiles + 1, 8, BR), F32)
    given, stays, to_p2, sums = call(
        second_kernel,
        [((6 * tiles, 8, BR), F32)] * 2 + [sent, ((everyone, 4, BR), F32)],
        *split, p2, p1, own, four[blocks:], b, there, conds, pads_sent, ones, ones_there, at_pads, sink, top,
        start_picked, start_product, start_jump, z, known, guide,
    )
    given = lax.ppermute(given, "sub", swap)
    to_e, to_o, own_part = call(sort_kernel, [sent, sent, pair_tiles], places, given, stays, top)
    to_e, to_o, to_p2 = barrier((to_e, to_o, to_p2))
    from_o = lax.ppermute(to_o, "sub", beside(count))
    from_e = lax.ppermute(to_e, "sub", [(i, i ^ 2) for i in range(count)])
    from_p2 = lax.ppermute(to_p2, "sub", far)
    all_sums = lax.all_to_all(sums, ("board", "sub"), 0, 0)
    from_o, from_e, from_p2, all_sums = barrier((from_o, from_e, from_p2, all_sums))
    (steps,) = call(steps_kernel, [((3, cases, BR), F32)], all_sums)
    solution, residual = call(
        end_kernel,
        [full, full],
        rhs[0], z, image, own, places, own_part, from_e, from_o, from_p2, top, steps,
    )
    return (solution[None], residual[None])


def solution(mesh):
    in_specs = (
        P("board", None, "sub"),
        P("board", "sub", None),
        P("board", "sub"),
        P("board", "sub"),
        P("board", "sub"),
        P("board", "sub"),
        P("board", "sub"),
    )
    out_specs = (P("board", None, "sub"), P("board", None, "sub"))
    return jax.shard_map(
        on_device, mesh=mesh, in_specs=in_specs, out_specs=out_specs, check_vma=False
    )
```

```python
import jax
import jax.numpy as jnp
from jax import lax
from jax.experimental import pallas as pl
from jax.experimental.pallas import tpu as pltpu
from jax.sharding import PartitionSpec as P

BR = 128
REACH = 3
F32 = jnp.float32
HALF = jnp.bfloat16
barrier = lax.optimization_barrier


def climb(count, step):
    pairs = []
    for source in range(count):
        chip, core = divmod(source, 2)
        target = chip - step if core else chip + step
        inside = 0 <= target < count // 2
        pairs.append((source, target * 2 + core if inside else source ^ 1))
    return pairs


def leap(count):
    pairs = []
    for source in range(count):
        chip, core = divmod(source, 2)
        target = chip + 2 if core else chip - 2
        if 0 <= target < count // 2:
            pairs.append((source, target * 2 + 1 - core))
        else:
            pairs.append((source, source ^ 2))
    return pairs


def beside(count):
    pairs = []
    for source in range(count):
        chip, core = divmod(source, 2)
        target = chip + 1 if chip % 2 else chip - 1
        inside = 0 <= target < count // 2
        pairs.append((source, target * 2 + core if inside else source ^ 1))
    return pairs


def turned(pairs):
    return [(target, source) for source, target in pairs]


def thirds(value):
    high = value.astype(HALF)
    rest = value - high.astype(F32)
    middle = rest.astype(HALF)
    return high, middle, (rest - middle.astype(F32)).astype(HALF)


def dot(left, right):
    return jnp.dot(left, right, preferred_element_type=F32)


def times_ones(value, ones, turn):
    rows = value.shape[0]
    parts = jnp.concatenate(thirds(value))
    if turn:
        out = lax.dot_general(parts, ones, (((1,), (1,)), ((), ())), preferred_element_type=F32)
    else:
        out = dot(parts, ones)
    return out[:rows] + (out[rows : 2 * rows] + out[2 * rows :])


def pad_matrix(pad_rows, owned):
    here = lax.broadcasted_iota(jnp.int32, (owned, pad_rows.shape[1]), 0)
    return (here == pad_rows).astype(F32).astype(HALF)


def product_of(value, high, middle, low):
    rows = value.shape[0]
    one, two, three = thirds(value)
    first = dot(jnp.concatenate([one, two, three]), high[...])
    second = dot(jnp.concatenate([one, two]), middle[...])
    small = first[2 * rows :] + second[rows:] + dot(one, low[...])
    return (small + (first[rows : 2 * rows] + second[:rows])) + first[:rows]


def wide(pair):
    return jnp.concatenate([pair[0], pair[1]], axis=1)


def put_wide(ref, start, value):
    ref[start] = value[:, :BR]
    ref[start + 1] = value[:, BR:]


def lanes_of(cases, slot):
    lane = lax.broadcasted_iota(jnp.int32, (cases, BR), 1)
    return lane == lax.broadcasted_iota(jnp.int32, (cases, BR), 0) + slot * cases


def as_column(row, slot, cases):
    return jnp.sum(jnp.where(lanes_of(cases, slot), row, 0.0), axis=1, keepdims=True)


def begin_kernel(z, pad_rows, pad_cond, ones_out, pads_out):
    cases = z.shape[0]
    owned, count = ones_out.shape
    ones = pad_matrix(pad_rows[...], owned)
    ones_out[...] = ones
    pads_out[...] = jnp.zeros_like(pads_out)
    pads_out[:cases, :count] = times_ones(z[...], ones, False)
    pads_out[cases : cases + 1, :count] = pad_cond[...]
    pads_out[cases + 8 : cases + 9, :count] = pad_rows[...].astype(F32)


def places_kernel(blocks, places):
    position = lax.axis_index("sub")
    chip, core = position // 2, lax.rem(position, 2)
    above, below = lax.axis_size("sub") // 2 - 1 - chip, chip
    touched = blocks.shape[1]
    listed = blocks[...]
    offset = listed // 2 - position
    mirrored = jnp.where(core == 0, offset, -offset)
    place = jnp.where(mirrored == 2, 6, jnp.where(mirrored == 3, 5, mirrored + REACH))
    place = place * 2 + lax.rem(listed, 2)
    spots = 2 * (2 * REACH + 1)
    for i in range(touched):
        here = jnp.broadcast_to(place[:, i : i + 1], places.shape[1:])
        for j in range(spots):
            places[i * spots + j] = (here == j).astype(F32)
    near = jnp.where(core == 0, above, below) >= 1
    far = jnp.where(core == 0, below, above) >= 2
    odd = lax.rem(chip, 2) == 1
    cross = jnp.where(odd, above, below) >= 1
    inner = odd == (core == 0)
    for i, sender in enumerate((near, far, cross, inner)):
        places[touched * spots + i] = jnp.full(places.shape[1:], sender.astype(F32))


def split_kernel(schur, high, middle, low, top, held, sems):
    chunk = held.shape[0] // sems.shape[0]
    copies = []
    for i in range(sems.shape[0]):
        rows = slice(i * chunk, (i + 1) * chunk)
        copies.append(pltpu.make_async_copy(schur.at[rows], held.at[rows], sems.at[i]))
    for copy in copies:
        copy.start()
    largest = jnp.ones((1, chunk), F32)
    for i, copy in enumerate(copies):
        rows = slice(i * chunk, (i + 1) * chunk)
        copy.wait()
        high[rows], middle[rows], low[rows] = thirds(0.25 * held[rows])
        largest = jnp.maximum(largest, jnp.max(held[rows, rows], axis=0, keepdims=True))
    top[...] = jnp.broadcast_to(jnp.max(largest, axis=1, keepdims=True), top.shape)


def spot(places, i, cases):
    return jnp.concatenate([places[i]] * (cases // 8))


def picked_blocks(places, held, touched):
    cases, spots = held[0].shape[0], len(held)
    picked = []
    for i in range(touched):
        total = spot(places, i * spots, cases) * held[0]
        for j in range(1, spots):
            total = total + spot(places, i * spots + j, cases) * held[j]
        picked.append(total)
    return jnp.concatenate(picked, axis=1)


def landed_blocks(places, product):
    cases, touched = product.shape[0], product.shape[1] // BR
    spots = (places.shape[0] - 4) // touched
    landed = []
    for j in range(spots):
        total = spot(places, j, cases) * product[:, :BR]
        for i in range(1, touched):
            total = total + spot(places, i * spots + j, cases) * product[:, i * BR : (i + 1) * BR]
        landed.append(total)
    return landed


def halves(*values):
    return [value[:, start : start + BR] for value in values for start in (0, BR)]


def held_blocks(p2, p1, own, a, b):
    return [p2[0], p2[1], p1[0], p1[1], p1[2], p1[3], own[0], own[1], a[0], a[1], b[0], b[1], b[2], b[3]]


def mean_of(mine, conds, cases, count):
    return 0.5 * (mine[cases : cases + 1, :count] + conds[cases : cases + 1, :count])


def first_kernel(
    places, high, middle, low, p2, p1, four, b, back, to_p1, to_p2, kept, picked_out, product_out
):
    touched = high.shape[0] // BR
    picked = picked_blocks(places, halves(p2, p1[0], p1[1], four[0], four[1], b[0], b[1]), touched)
    product = product_of(4.0 * picked, high, middle, low)
    landed = landed_blocks(places, product)
    for j in range(2):
        to_p2[j] = landed[j]
    for j in range(4):
        back[j] = landed[10 + j]
        to_p1[j] = landed[2 + j]
    for j in range(4):
        kept[j] = landed[6 + j]
    picked_out[...] = picked
    product_out[...] = product


def ties_kernel(z, mine, conds, ones, sink, local, jump_out, ones_there):
    cases, count = z.shape[0], ones.shape[1]
    jump = mine[:cases, :count] - conds[:cases, :count]
    jump_out[...] = jump
    pads = conds[cases + 8 : cases + 9, :count].astype(jnp.int32)
    ones_there[...] = pad_matrix(pads, z.shape[1])
    local[...] = sink[...] * z[...] + times_ones(mean_of(mine, conds, cases, count) * jump, ones[...], True)


def folded(value):
    total = value[:, :BR]
    for i in range(1, value.shape[1] // BR):
        total = total + value[:, i * BR : (i + 1) * BR]
    return total


def across_lanes(value):
    return jnp.sum(value, axis=1, keepdims=True)


def largest_of(blocks, pads):
    size = jnp.maximum(
        jnp.max(jnp.abs(blocks), axis=1, keepdims=True), jnp.max(jnp.abs(pads), axis=1, keepdims=True)
    )
    return jnp.where(size > 0.0, size, 1.0)


def case_row(columns):
    cases = columns[0].shape[0]
    total = jnp.where(lanes_of(cases, 0), columns[0], 0.0)
    for slot in range(1, len(columns)):
        total = jnp.where(lanes_of(cases, slot), columns[slot], total)
    return jnp.sum(total, axis=0, keepdims=True)


def shares_kernel(
    rhs, z, image, scaled, ones, precond, sink, picked, product, jump, mine, conds, top, known, guide, at_pads
):
    cases, count = jump.shape
    at_pads[...] = times_ones(wide(scaled), ones[...], False)
    start = z[...]
    bulk = 0.25 * (4.0 / top[0:1, 0:1])
    mean = mean_of(mine, conds, cases, count)
    size = largest_of(picked[...], jump[...])
    inverse = 1.0 / size
    unit = picked[...] * inverse
    unit_jump = jump[...] * inverse
    unit_own = start * inverse
    pulled = (product[...] * bulk) * inverse
    energy = across_lanes(folded(unit * pulled) + bulk * folded(sink[...] * unit_own * unit_own))
    energy = energy + 0.5 * bulk * across_lanes(mean * unit_jump * unit_jump)
    norm = across_lanes(folded(rhs[...] * start))
    curve = across_lanes(folded(start * image[...]))
    reach = jnp.max(jnp.abs(image[...]), axis=1, keepdims=True)
    still = reach <= 0.0
    scale = jnp.clip(size / jnp.where(still, 1.0, reach), 1e-34, 1e30)
    guess = jnp.where(curve > 0.0, norm / jnp.where(curve > 0.0, curve, 1.0), 0.0)
    guess = jnp.where(still, 1.0, jnp.clip(guess, scale * (1.0 / 1024.0), scale * 8.0))
    moved = guess * image[...]
    rest = rhs[...] - moved
    weighted = precond[...] * moved
    known[0:1] = case_row([norm, guess, across_lanes(folded(precond[...] * rest * rest)), across_lanes(folded(weighted * rest))])
    known[1:2] = case_row(
        [across_lanes(folded(weighted * moved)), size, energy, jnp.broadcast_to(top[0:1, 0:1], size.shape)]
    )
    tilt = jnp.where(norm > 0.0, curve / jnp.where(norm > 0.0, norm, 1.0), 0.0) * size
    guide[0] = jnp.broadcast_to(jnp.clip(tilt, -1e37, 1e37), guide.shape[1:])
    guide[1] = jnp.broadcast_to(inverse, guide.shape[1:])


def put_tiles(ref, start, block):
    tiles = block.shape[0] // 8
    ref[start * tiles : (start + 1) * tiles] = block.reshape(tiles, 8, BR)


def second_kernel(
    places, high, middle, low, p2, p1, own, a, b, there, conds, mine, ones, ones_there, at_pads, sink, top,
    start_picked, start_product, start_jump, start_own, known, guide,
    given, stays, to_p2, sums,
):
    touched = high.shape[0] // BR
    cases = own.shape[1]
    count = ones.shape[1]
    less = 4.0 / top[0:1, 0:1]
    picked = picked_blocks(places, held_blocks(p2, p1, own, a, b), touched)
    product = product_of((picked * less) * (1.0 / 1024.0), high, middle, low)
    here = wide(own)
    jump = at_pads[...] - times_ones(wide(there[0:2]), ones_there[...], False)
    mean = mean_of(mine, conds, cases, count)
    local = sink[...] * here + times_ones(mean * jump, ones[...], True)
    local = (local * less) * (1.0 / 4096.0)
    size = largest_of(picked, jump)
    inverse = 1.0 / size
    bulk = 0.25 * less
    tilt = jnp.clip(guide[0, :, 0:1] * inverse, -1e3, 1e3)
    unit = guide[1, :, 0:1]
    tilted = tilt * unit
    rest = picked * inverse - tilted * start_picked[...]
    pulled = product * (1024.0 * inverse) - (start_product[...] * bulk) * tilted
    rest_own = here * inverse - tilted * start_own[...]
    rest_jump = jump * inverse - tilted * start_jump[...]
    sunk = sink[...] * rest_own
    tied = 0.5 * mean * rest_jump
    tail = jnp.zeros((cases, BR - count), F32)
    energy = folded(rest * pulled) + bulk * folded(sunk * rest_own)
    energy = energy + bulk * jnp.concatenate([tied * rest_jump, tail], axis=1)
    cross = folded(start_picked[...] * unit * pulled) + bulk * folded(sunk * (start_own[...] * unit))
    cross = cross + bulk * jnp.concatenate([tied * (start_jump[...] * unit), tail], axis=1)
    own_row = case_row([size, tilt, across_lanes(cross), across_lanes(energy)])
    total = jnp.concatenate([known[0:2], own_row, jnp.zeros_like(own_row)])
    sums[...] = jnp.broadcast_to(total[None], sums.shape)
    landed = landed_blocks(places, product)
    for j in range(2):
        put_tiles(to_p2, j, landed[j])
        put_tiles(given, j, landed[4 + j])
        put_tiles(given, 2 + j, landed[10 + j])
        put_tiles(given, 4 + j, landed[8 + j])
        put_tiles(stays, j, landed[2 + j])
        put_tiles(stays, 2 + j, landed[12 + j])
        put_tiles(stays, 4 + j, landed[6 + j] + local[:, j * BR : (j + 1) * BR])
    to_p2[to_p2.shape[0] - 1] = top[...]


def part_kernel(places, kept, local, from_p1, from_p2, precond, top, part):
    cases = kept.shape[1]
    near, far = [spot(places, places.shape[0] - 4 + i, cases)[None] for i in range(2)]
    one = from_p1[...] * near
    mine = kept[0:2] + one[0:2] + from_p2[...] * far
    part[0] = mine[0] + local[:, :BR]
    part[1] = mine[1] + local[:, BR:]
    part[2:4] = kept[2:4] + one[2:4]
    part[4] = jnp.zeros(part.shape[1:], F32)
    part[4, 0:1] = precond[:, :BR]
    part[4, 1:2] = precond[:, BR:]
    part[4, 8:16] = top[...]


def turn_kernel(part, there, precond, image_out, both_out, own_out, top_out):
    image = wide(part[0:2] + there[2:4])
    other = part[2:4] + there[0:2]
    image_out[...] = image
    scaled = precond[...] * image
    put_wide(both_out, 0, scaled)
    put_wide(own_out, 0, scaled)
    both_out[2] = there[4, 0:1] * other[0]
    both_out[3] = there[4, 1:2] * other[1]
    top_out[...] = jnp.maximum(part[4, 8:16], there[4, 8:16])


def sort_kernel(places, given, stays, top, to_e, to_o, own):
    pair = stays.shape[0] // 3
    inner = places[places.shape[0] - 1] > 0.0
    for i in range(pair):
        near = stays[i] + given[pair + i]
        away = stays[pair + i] + given[i]
        to_e[i] = jnp.where(inner, near, away)
        to_o[i] = jnp.where(inner, away, near)
        own[i] = stays[2 * pair + i] + given[2 * pair + i]
    to_e[pair] = top[...]
    to_o[pair] = top[...]


def steps_kernel(sums, steps):
    cases = steps.shape[1]
    rows = [sums[:, i, :] for i in range(3)]

    def value(i):
        row = rows[i // 4]
        return row if i % 4 == 0 else pltpu.roll(row, BR - (i % 4) * cases, 1)

    norm, guess, rest, mixed, moved, size, energy, top, other_size, tilt, cross, other_energy = [
        value(i) for i in range(12)
    ]

    def everyone(terms):
        return jnp.sum(terms, axis=0, keepdims=True)

    norm = everyone(norm)
    alpha = norm / everyone((size * size * energy) * top)
    shift = alpha / guess - 1.0
    fresh = everyone(rest + shift * (shift * moved - 2.0 * mixed))
    grown = 1.0 + fresh / norm
    two = alpha * other_size
    one = grown * size - two * tilt
    bend = everyone(((one * one) * energy + two * (two * other_energy - 2.0 * one * cross)) * top)
    for i, row in enumerate((alpha, grown, fresh / bend)):
        steps[i] = jnp.broadcast_to(as_column(row, 0, cases), steps.shape[1:])


def end_kernel(rhs, z, image, scaled, places, own, from_e, from_o, from_p2, top, steps, solution, residual):
    cases = solution.shape[0]
    tiles = cases // 8
    alpha, grown, step = [wide([steps[i], steps[i]]) for i in range(3)]
    start = z[...]
    direction = grown * start - alpha * wide(scaled)
    solution[...] = alpha * start + step * direction
    one = jnp.ones_like(top)
    cross, far = places[places.shape[0] - 2], places[places.shape[0] - 3]
    parts = [(own, top[...], one)] + [
        (part, part[2 * tiles], valid) for part, valid in ((from_e, one), (from_o, cross), (from_p2, far))
    ]
    most = top[...]
    for _, scale, valid in parts[1:]:
        most = jnp.maximum(most, valid * scale)
    total = 0.0
    for part, scale, valid in parts:
        factor = valid * (scale / most)
        total = total + part[: 2 * tiles] * factor[None]
    blocks = total.reshape(2, cases, BR)
    bulk = spot([most], 0, cases)
    second = ((alpha * wide(blocks)) * wide([bulk, bulk])) * 1024.0
    residual[...] = rhs[...] - alpha * image[...] - step * (grown * image[...] - second)


def call(kernel, outs, *operands, scratch=(), far=(), grant=32):
    def space(outside, i):
        return pl.BlockSpec(memory_space=pl.ANY if i in outside else pltpu.VMEM)

    return pl.pallas_call(
        kernel,
        in_specs=[space(far, i) for i in range(len(operands))],
        out_specs=[space((), i) for i in range(len(outs))],
        out_shape=[jax.ShapeDtypeStruct(shape, kind) for shape, kind in outs],
        scratch_shapes=list(scratch),
        compiler_params=pltpu.CompilerParams(vmem_limit_bytes=grant * 1024 * 1024),
    )(*operands)


def on_device(rhs, schur, block_list, pad_rows, pad_cond, sink, precond):
    matrix = schur[0]
    cases, owned = rhs.shape[1:]
    inner = matrix.shape[0]
    blocks = owned // BR
    touched = inner // BR
    count = lax.axis_size("sub")
    everyone = count * lax.axis_size("board")
    pads = pad_rows.shape[1]
    swap = [(i, i ^ 1) for i in range(count)]
    across = [(i, i ^ 1) for i in range(lax.axis_size("board"))]
    near, far = climb(count, 1), leap(count)
    pair = ((blocks, cases, BR), F32)
    both = ((2 * blocks, cases, BR), F32)
    tile = ((8, BR), F32)
    full = ((cases, owned), F32)
    semaphores = pltpu.SemaphoreType.DMA

    z = barrier(precond * rhs[0])
    ones, pads_sent = call(begin_kernel, [((owned, pads), HALF), ((4 * cases + 8, BR), F32)], z, pad_rows, pad_cond)
    chunks = touched
    spots = 2 * (2 * REACH + 1)
    (places,) = call(places_kernel, [((touched * spots + 4, 8, BR), F32)], block_list)
    high, middle, low, top = call(
        split_kernel,
        [((inner, inner), HALF)] * 3 + [tile],
        matrix,
        far=range(1),
        scratch=[pltpu.VMEM((inner, inner), F32), semaphores((chunks,))],
        grant=49,
    )

    def collect(back, to_p1, to_p2):
        from_p2 = lax.ppermute(to_p2, "sub", far)
        to_p1 = to_p1 + lax.ppermute(back, "sub", swap)
        return to_p1, from_p2

    scale_there = lax.ppermute(precond, "sub", swap)
    four = barrier(jnp.stack([z, scale_there * lax.ppermute(rhs[0], "sub", swap)]))
    p2 = lax.ppermute(z, "sub", far)
    p1 = lax.ppermute(four, "sub", near)
    p1, p2, high, middle, low, top = barrier((p1, p2, high, middle, low, top))
    b = lax.ppermute(p1, "sub", swap)
    b, ones, pads_sent = barrier((b, ones, pads_sent))
    split = (places, high, middle, low)
    back, to_p1, to_p2, kept, start_picked, start_product = call(
        first_kernel,
        [both, both, pair, both, ((cases, inner), F32), ((cases, inner), F32)],
        *split, p2, p1, four, b,
    )
    conds = lax.ppermute(pads_sent, "board", across)
    local, start_jump, ones_there = call(
        ties_kernel,
        [full, ((cases, pads), F32), ((owned, pads), HALF)],
        z, pads_sent, conds, ones, sink,
    )
    to_p1, from_p2 = collect(back, to_p1, to_p2)
    from_p1 = lax.ppermute(to_p1, "sub", turned(near))
    (part,) = call(part_kernel, [((2 * blocks + 1, cases, BR), F32)], places, kept, local, from_p1, from_p2, precond, top)
    part_there = lax.ppermute(part, "sub", swap)
    image, four, own, top = call(turn_kernel, [full, both, pair, tile], part, part_there, precond)
    known, guide, at_pads = call(
        shares_kernel,
        [((2, BR), F32), ((2, cases, BR), F32), ((cases, pads), F32)],
        rhs[0], z, image, own, ones, precond, sink, start_picked, start_product, start_jump, pads_sent, conds, top,
    )
    p1 = lax.ppermute(four, "sub", near)
    p2 = lax.ppermute(own, "sub", far)
    there = lax.ppermute(four, "board", across)
    p1, p2, known, guide, at_pads = barrier((p1, p2, known, guide, at_pads))
    b = lax.ppermute(p1, "sub", swap)
    tiles = cases // 8
    pair_tiles = ((2 * tiles, 8, BR), F32)
    sent = ((2 * tiles + 1, 8, BR), F32)
    given, stays, to_p2, sums = call(
        second_kernel,
        [((6 * tiles, 8, BR), F32)] * 2 + [sent, ((everyone, 4, BR), F32)],
        *split, p2, p1, own, four[blocks:], b, there, conds, pads_sent, ones, ones_there, at_pads, sink, top,
        start_picked, start_product, start_jump, z, known, guide,
    )
    given = lax.ppermute(given, "sub", swap)
    to_e, to_o, own_part = call(sort_kernel, [sent, sent, pair_tiles], places, given, stays, top)
    to_e, to_o, to_p2 = barrier((to_e, to_o, to_p2))
    from_o = lax.ppermute(to_o, "sub", beside(count))
    from_e = lax.ppermute(to_e, "sub", [(i, i ^ 2) for i in range(count)])
    from_p2 = lax.ppermute(to_p2, "sub", far)
    all_sums = lax.all_to_all(sums, ("board", "sub"), 0, 0)
    from_o, from_e, from_p2, all_sums = barrier((from_o, from_e, from_p2, all_sums))
    (steps,) = call(steps_kernel, [((3, cases, BR), F32)], all_sums)
    solution, residual = call(
        end_kernel,
        [full, full],
        rhs[0], z, image, own, places, own_part, from_e, from_o, from_p2, top, steps,
    )
    return (solution[None], residual[None])


def solution(mesh):
    in_specs = (
        P("board", None, "sub"),
        P("board", "sub", None),
        P("board", "sub"),
        P("board", "sub"),
        P("board", "sub"),
        P("board", "sub"),
        P("board", "sub"),
    )
    out_specs = (P("board", None, "sub"), P("board", None, "sub"))
    return jax.shard_map(
        on_device, mesh=mesh, in_specs=in_specs, out_specs=out_specs, check_vma=False
    )
```

```python
import jax
import jax.numpy as jnp
from jax import lax
from jax.experimental import pallas as pl
from jax.experimental.pallas import tpu as pltpu
from jax.sharding import PartitionSpec as P

BR = 128
REACH = 3
F32 = jnp.float32
HALF = jnp.bfloat16
barrier = lax.optimization_barrier


def climb(count, step):
    pairs = []
    for source in range(count):
        chip, core = divmod(source, 2)
        target = chip - step if core else chip + step
        inside = 0 <= target < count // 2
        pairs.append((source, target * 2 + core if inside else source ^ 1))
    return pairs


def leap(count):
    pairs = []
    for source in range(count):
        chip, core = divmod(source, 2)
        target = chip + 2 if core else chip - 2
        if 0 <= target < count // 2:
            pairs.append((source, target * 2 + 1 - core))
        else:
            pairs.append((source, source ^ 2))
    return pairs


def beside(count):
    pairs = []
    for source in range(count):
        chip, core = divmod(source, 2)
        target = chip + 1 if chip % 2 else chip - 1
        inside = 0 <= target < count // 2
        pairs.append((source, target * 2 + core if inside else source ^ 1))
    return pairs


def turned(pairs):
    return [(target, source) for source, target in pairs]


def thirds(value):
    high = value.astype(HALF)
    rest = value - high.astype(F32)
    middle = rest.astype(HALF)
    return high, middle, (rest - middle.astype(F32)).astype(HALF)


def dot(left, right):
    return jnp.dot(left, right, preferred_element_type=F32)


def times_ones(value, ones, turn):
    rows = value.shape[0]
    parts = jnp.concatenate(thirds(value))
    if turn:
        out = lax.dot_general(parts, ones, (((1,), (1,)), ((), ())), preferred_element_type=F32)
    else:
        out = dot(parts, ones)
    return out[:rows] + (out[rows : 2 * rows] + out[2 * rows :])


def pad_matrix(pad_rows, owned):
    here = lax.broadcasted_iota(jnp.int32, (owned, pad_rows.shape[1]), 0)
    return (here == pad_rows).astype(F32).astype(HALF)


def product_of(value, high, middle, low):
    rows = value.shape[0]
    one, two, three = thirds(value)
    first = dot(jnp.concatenate([one, two, three]), high[...])
    second = dot(jnp.concatenate([one, two]), middle[...])
    small = first[2 * rows :] + second[rows:] + dot(one, low[...])
    return (small + (first[rows : 2 * rows] + second[:rows])) + first[:rows]


def wide(pair):
    return jnp.concatenate([pair[0], pair[1]], axis=1)


def put_wide(ref, start, value):
    ref[start] = value[:, :BR]
    ref[start + 1] = value[:, BR:]


def lanes_of(cases, slot):
    lane = lax.broadcasted_iota(jnp.int32, (cases, BR), 1)
    return lane == lax.broadcasted_iota(jnp.int32, (cases, BR), 0) + slot * cases


def as_column(row, slot, cases):
    return jnp.sum(jnp.where(lanes_of(cases, slot), row, 0.0), axis=1, keepdims=True)


def begin_kernel(z, pad_rows, pad_cond, ones_out, pads_out):
    cases = z.shape[0]
    owned, count = ones_out.shape
    ones = pad_matrix(pad_rows[...], owned)
    ones_out[...] = ones
    pads_out[...] = jnp.zeros_like(pads_out)
    pads_out[:cases, :count] = times_ones(z[...], ones, False)
    pads_out[cases : cases + 1, :count] = pad_cond[...]
    pads_out[cases + 8 : cases + 9, :count] = pad_rows[...].astype(F32)


def places_kernel(blocks, places):
    position = lax.axis_index("sub")
    chip, core = position // 2, lax.rem(position, 2)
    above, below = lax.axis_size("sub") // 2 - 1 - chip, chip
    touched = blocks.shape[1]
    listed = blocks[...]
    offset = listed // 2 - position
    mirrored = jnp.where(core == 0, offset, -offset)
    place = jnp.where(mirrored == 2, 6, jnp.where(mirrored == 3, 5, mirrored + REACH))
    place = place * 2 + lax.rem(listed, 2)
    spots = 2 * (2 * REACH + 1)
    for i in range(touched):
        here = jnp.broadcast_to(place[:, i : i + 1], places.shape[1:])
        for j in range(spots):
            places[i * spots + j] = (here == j).astype(F32)
    near = jnp.where(core == 0, above, below) >= 1
    far = jnp.where(core == 0, below, above) >= 2
    odd = lax.rem(chip, 2) == 1
    cross = jnp.where(odd, above, below) >= 1
    inner = odd == (core == 0)
    for i, sender in enumerate((near, far, cross, inner)):
        places[touched * spots + i] = jnp.full(places.shape[1:], sender.astype(F32))


def split_kernel(schur, high, middle, low, top, held, sems):
    chunk = held.shape[0] // sems.shape[0]
    copies = []
    for i in range(sems.shape[0]):
        rows = slice(i * chunk, (i + 1) * chunk)
        copies.append(pltpu.make_async_copy(schur.at[rows], held.at[rows], sems.at[i]))
    for copy in copies:
        copy.start()
    largest = jnp.ones((1, chunk), F32)
    for i, copy in enumerate(copies):
        rows = slice(i * chunk, (i + 1) * chunk)
        copy.wait()
        high[rows], middle[rows], low[rows] = thirds(0.25 * held[rows])
        largest = jnp.maximum(largest, jnp.max(held[rows, rows], axis=0, keepdims=True))
    top[...] = jnp.broadcast_to(jnp.max(largest, axis=1, keepdims=True), top.shape)


def late_kernel(blocks, high, middle, low, late_high, late_middle, late_low):
    position = lax.axis_index("sub")
    core = lax.rem(position, 2)
    touched = blocks.shape[1]
    spots = []
    for i in range(touched):
        offset = blocks[0, i] // 2 - position
        mirrored = jnp.where(core == 0, offset, -offset)
        place = jnp.where(mirrored == 2, 6, jnp.where(mirrored == 3, 5, mirrored + REACH))
        spots.append(place * 2 + lax.rem(blocks[0, i], 2))
    for j in range(LATE):
        source = jnp.int32(-1)
        for i in range(touched):
            source = jnp.where(spots[i] == SPOTS - LATE + j, i, source)
        rows = pl.ds(pl.multiple_of(jnp.maximum(source, 0) * BR, BR), BR)
        keep = jnp.where(source >= 0, 1.0, 0.0)
        for part, late in ((high, late_high), (middle, late_middle), (low, late_low)):
            late[j * BR : (j + 1) * BR] = (part[rows].astype(F32) * keep).astype(HALF)


def spot(places, i, cases):
    return jnp.concatenate([places[i]] * (cases // 8))


SPOTS = 2 * (2 * REACH + 1)
LATE = 4


def picked_blocks(places, held, touched, begin):
    cases = held[0].shape[0]
    picked = []
    for i in range(touched):
        total = spot(places, i * SPOTS + begin, cases) * held[0]
        for j in range(1, len(held)):
            total = total + spot(places, i * SPOTS + begin + j, cases) * held[j]
        picked.append(total)
    return jnp.concatenate(picked, axis=1)


def landed_blocks(places, product):
    cases, touched = product.shape[0], product.shape[1] // BR
    spots = (places.shape[0] - 4) // touched
    landed = []
    for j in range(spots):
        total = spot(places, j, cases) * product[:, :BR]
        for i in range(1, touched):
            total = total + spot(places, i * spots + j, cases) * product[:, i * BR : (i + 1) * BR]
        landed.append(total)
    return landed


def halves(*values):
    return [value[:, start : start + BR] for value in values for start in (0, BR)]


def mean_of(mine, conds, cases, count):
    return 0.5 * (mine[cases : cases + 1, :count] + conds[cases : cases + 1, :count])


def first_kernel(
    places, high, middle, low, p2, p1, four, b, back, to_p1, to_p2, kept, picked_out, product_out
):
    picked = picked_blocks(places, halves(p2, p1[0], p1[1], four[0], four[1], b[0], b[1]), high.shape[0] // BR, 0)
    product = product_of(4.0 * picked, high, middle, low)
    landed = landed_blocks(places, product)
    for j in range(2):
        to_p2[j] = landed[j]
    for j in range(4):
        back[j] = landed[10 + j]
        to_p1[j] = landed[2 + j]
    for j in range(4):
        kept[j] = landed[6 + j]
    picked_out[...] = picked
    product_out[...] = product


def ties_kernel(z, mine, conds, ones, sink, local, jump_out, ones_there):
    cases, count = z.shape[0], ones.shape[1]
    jump = mine[:cases, :count] - conds[:cases, :count]
    jump_out[...] = jump
    pads = conds[cases + 8 : cases + 9, :count].astype(jnp.int32)
    ones_there[...] = pad_matrix(pads, z.shape[1])
    local[...] = sink[...] * z[...] + times_ones(mean_of(mine, conds, cases, count) * jump, ones[...], True)


def folded(value):
    total = value[:, :BR]
    for i in range(1, value.shape[1] // BR):
        total = total + value[:, i * BR : (i + 1) * BR]
    return total


def across_lanes(value):
    return jnp.sum(value, axis=1, keepdims=True)


def largest_of(blocks, pads):
    size = jnp.maximum(
        jnp.max(jnp.abs(blocks), axis=1, keepdims=True), jnp.max(jnp.abs(pads), axis=1, keepdims=True)
    )
    return jnp.where(size > 0.0, size, 1.0)


def case_row(columns):
    cases = columns[0].shape[0]
    total = jnp.where(lanes_of(cases, 0), columns[0], 0.0)
    for slot in range(1, len(columns)):
        total = jnp.where(lanes_of(cases, slot), columns[slot], total)
    return jnp.sum(total, axis=0, keepdims=True)


def shares_kernel(
    rhs, z, image, scaled, ones, precond, sink, picked, product, jump, mine, conds, top, known, guide, at_pads
):
    cases, count = jump.shape
    at_pads[...] = times_ones(wide(scaled), ones[...], False)
    start = z[...]
    bulk = 0.25 * (4.0 / top[0:1, 0:1])
    mean = mean_of(mine, conds, cases, count)
    size = largest_of(picked[...], jump[...])
    inverse = 1.0 / size
    unit = picked[...] * inverse
    unit_jump = jump[...] * inverse
    unit_own = start * inverse
    pulled = (product[...] * bulk) * inverse
    energy = across_lanes(folded(unit * pulled) + bulk * folded(sink[...] * unit_own * unit_own))
    energy = energy + 0.5 * bulk * across_lanes(mean * unit_jump * unit_jump)
    norm = across_lanes(folded(rhs[...] * start))
    curve = across_lanes(folded(start * image[...]))
    reach = jnp.max(jnp.abs(image[...]), axis=1, keepdims=True)
    still = reach <= 0.0
    scale = jnp.clip(size / jnp.where(still, 1.0, reach), 1e-34, 1e30)
    guess = jnp.where(curve > 0.0, norm / jnp.where(curve > 0.0, curve, 1.0), 0.0)
    guess = jnp.where(still, 1.0, jnp.clip(guess, scale * (1.0 / 1024.0), scale * 8.0))
    moved = guess * image[...]
    rest = rhs[...] - moved
    weighted = precond[...] * moved
    known[0:1] = case_row([norm, guess, across_lanes(folded(precond[...] * rest * rest)), across_lanes(folded(weighted * rest))])
    known[1:2] = case_row(
        [across_lanes(folded(weighted * moved)), size, energy, jnp.broadcast_to(top[0:1, 0:1], size.shape)]
    )
    tilt = jnp.where(norm > 0.0, curve / jnp.where(norm > 0.0, norm, 1.0), 0.0) * size
    guide[0] = jnp.broadcast_to(jnp.clip(tilt, -1e37, 1e37), guide.shape[1:])
    guide[1] = jnp.broadcast_to(inverse, guide.shape[1:])


def put_tiles(ref, start, block):
    tiles = block.shape[0] // 8
    ref[start * tiles : (start + 1) * tiles] = block.reshape(tiles, 8, BR)


def second_early_kernel(places, high, middle, low, p2, p1, own, a, top, picked_out, product_out):
    held = [p2[0], p2[1], p1[0], p1[1], p1[2], p1[3], own[0], own[1], a[0], a[1]]
    picked = picked_blocks(places, held, high.shape[0] // BR, 0)
    picked_out[...] = picked
    product_out[...] = product_of((picked * (4.0 / top[0:1, 0:1])) * (1.0 / 1024.0), high, middle, low)


def second_kernel(
    places, high, middle, low, own, b, early, early_product, there, conds, mine, ones, ones_there, at_pads, sink, top,
    start_picked, start_product, start_jump, start_own, known, guide,
    given, stays, to_p2, sums,
):
    cases = own.shape[1]
    count = ones.shape[1]
    less = 4.0 / top[0:1, 0:1]
    held = [b[j] for j in range(LATE)]
    picked = early[...] + picked_blocks(places, held, early.shape[1] // BR, SPOTS - LATE)
    late = (jnp.concatenate(held, axis=1) * less) * (1.0 / 1024.0)
    product = early_product[...] + product_of(late, high, middle, low)
    scales = jnp.concatenate([there[4, 0:1], there[4, 1:2]], axis=1)
    values = scales * wide(there[0:2] + b[4:6])
    here = wide(own)
    jump = at_pads[...] - times_ones(values, ones_there[...], False)
    mean = mean_of(mine, conds, cases, count)
    local = sink[...] * here + times_ones(mean * jump, ones[...], True)
    local = (local * less) * (1.0 / 4096.0)
    size = largest_of(picked, jump)
    inverse = 1.0 / size
    bulk = 0.25 * less
    tilt = jnp.clip(guide[0, :, 0:1] * inverse, -1e3, 1e3)
    unit = guide[1, :, 0:1]
    tilted = tilt * unit
    rest = picked * inverse - tilted * start_picked[...]
    pulled = product * (1024.0 * inverse) - (start_product[...] * bulk) * tilted
    rest_own = here * inverse - tilted * start_own[...]
    rest_jump = jump * inverse - tilted * start_jump[...]
    sunk = sink[...] * rest_own
    tied = 0.5 * mean * rest_jump
    tail = jnp.zeros((cases, BR - count), F32)
    energy = folded(rest * pulled) + bulk * folded(sunk * rest_own)
    energy = energy + bulk * jnp.concatenate([tied * rest_jump, tail], axis=1)
    cross = folded(start_picked[...] * unit * pulled) + bulk * folded(sunk * (start_own[...] * unit))
    cross = cross + bulk * jnp.concatenate([tied * (start_jump[...] * unit), tail], axis=1)
    own_row = case_row([size, tilt, across_lanes(cross), across_lanes(energy)])
    total = jnp.concatenate([known[0:2], own_row, jnp.zeros_like(own_row)])
    sums[...] = jnp.broadcast_to(total[None], sums.shape)
    landed = landed_blocks(places, product)
    for j in range(2):
        put_tiles(to_p2, j, landed[j])
        put_tiles(given, j, landed[4 + j])
        put_tiles(given, 2 + j, landed[10 + j])
        put_tiles(given, 4 + j, landed[8 + j])
        put_tiles(stays, j, landed[2 + j])
        put_tiles(stays, 2 + j, landed[12 + j])
        put_tiles(stays, 4 + j, landed[6 + j] + local[:, j * BR : (j + 1) * BR])
    to_p2[to_p2.shape[0] - 1] = top[...]


def part_kernel(places, kept, local, from_p1, from_p2, precond, top, part):
    cases = kept.shape[1]
    near, far = [spot(places, places.shape[0] - 4 + i, cases)[None] for i in range(2)]
    one = from_p1[...] * near
    mine = kept[0:2] + one[0:2] + from_p2[...] * far
    part[0] = mine[0] + local[:, :BR]
    part[1] = mine[1] + local[:, BR:]
    part[2:4] = kept[2:4] + one[2:4]
    part[4] = jnp.zeros(part.shape[1:], F32)
    part[4, 0:1] = precond[:, :BR]
    part[4, 1:2] = precond[:, BR:]
    part[4, 8:16] = top[...]


def turn_kernel(part, there, precond, image_out, both_out, own_out, top_out):
    image = wide(part[0:2] + there[2:4])
    other = part[2:4] + there[0:2]
    image_out[...] = image
    scaled = precond[...] * image
    put_wide(both_out, 0, scaled)
    put_wide(own_out, 0, scaled)
    both_out[2] = there[4, 0:1] * other[0]
    both_out[3] = there[4, 1:2] * other[1]
    top_out[...] = jnp.maximum(part[4, 8:16], there[4, 8:16])


def sort_kernel(places, given, stays, top, to_e, to_o, own):
    pair = stays.shape[0] // 3
    inner = places[places.shape[0] - 1] > 0.0
    for i in range(pair):
        near = stays[i] + given[pair + i]
        away = stays[pair + i] + given[i]
        to_e[i] = jnp.where(inner, near, away)
        to_o[i] = jnp.where(inner, away, near)
        own[i] = stays[2 * pair + i] + given[2 * pair + i]
    to_e[pair] = top[...]
    to_o[pair] = top[...]


def steps_kernel(sums, steps):
    cases = steps.shape[1]
    rows = [sums[:, i, :] for i in range(3)]

    def value(i):
        row = rows[i // 4]
        return row if i % 4 == 0 else pltpu.roll(row, BR - (i % 4) * cases, 1)

    norm, guess, rest, mixed, moved, size, energy, top, other_size, tilt, cross, other_energy = [
        value(i) for i in range(12)
    ]

    def everyone(terms):
        return jnp.sum(terms, axis=0, keepdims=True)

    norm = everyone(norm)
    alpha = norm / everyone((size * size * energy) * top)
    shift = alpha / guess - 1.0
    fresh = everyone(rest + shift * (shift * moved - 2.0 * mixed))
    grown = 1.0 + fresh / norm
    two = alpha * other_size
    one = grown * size - two * tilt
    bend = everyone(((one * one) * energy + two * (two * other_energy - 2.0 * one * cross)) * top)
    for i, row in enumerate((alpha, grown, fresh / bend)):
        steps[i] = jnp.broadcast_to(as_column(row, 0, cases), steps.shape[1:])


def end_kernel(rhs, z, image, scaled, places, own, from_e, from_o, from_p2, top, steps, solution, residual):
    cases = solution.shape[0]
    tiles = cases // 8
    alpha, grown, step = [wide([steps[i], steps[i]]) for i in range(3)]
    start = z[...]
    direction = grown * start - alpha * wide(scaled)
    solution[...] = alpha * start + step * direction
    one = jnp.ones_like(top)
    cross, far = places[places.shape[0] - 2], places[places.shape[0] - 3]
    parts = [(own, top[...], one)] + [
        (part, part[2 * tiles], valid) for part, valid in ((from_e, one), (from_o, cross), (from_p2, far))
    ]
    most = top[...]
    for _, scale, valid in parts[1:]:
        most = jnp.maximum(most, valid * scale)
    total = 0.0
    for part, scale, valid in parts:
        factor = valid * (scale / most)
        total = total + part[: 2 * tiles] * factor[None]
    blocks = total.reshape(2, cases, BR)
    bulk = spot([most], 0, cases)
    second = ((alpha * wide(blocks)) * wide([bulk, bulk])) * 1024.0
    residual[...] = rhs[...] - alpha * image[...] - step * (grown * image[...] - second)


def call(kernel, outs, *operands, scratch=(), far=(), scalar=(), grant=32):
    def space(outside, i):
        return pl.BlockSpec(memory_space=pl.ANY if i in outside else pltpu.VMEM)

    return pl.pallas_call(
        kernel,
        in_specs=[pl.BlockSpec(memory_space=pltpu.SMEM) if i in scalar else space(far, i) for i in range(len(operands))],
        out_specs=[space((), i) for i in range(len(outs))],
        out_shape=[jax.ShapeDtypeStruct(shape, kind) for shape, kind in outs],
        scratch_shapes=list(scratch),
        compiler_params=pltpu.CompilerParams(vmem_limit_bytes=grant * 1024 * 1024),
    )(*operands)


def on_device(rhs, schur, block_list, pad_rows, pad_cond, sink, precond):
    matrix = schur[0]
    cases, owned = rhs.shape[1:]
    inner = matrix.shape[0]
    blocks = owned // BR
    touched = inner // BR
    count = lax.axis_size("sub")
    everyone = count * lax.axis_size("board")
    pads = pad_rows.shape[1]
    swap = [(i, i ^ 1) for i in range(count)]
    across = [(i, i ^ 1) for i in range(lax.axis_size("board"))]
    near, far = climb(count, 1), leap(count)
    pair = ((blocks, cases, BR), F32)
    both = ((2 * blocks, cases, BR), F32)
    tile = ((8, BR), F32)
    full = ((cases, owned), F32)
    semaphores = pltpu.SemaphoreType.DMA

    z = barrier(precond * rhs[0])
    ones, pads_sent = call(begin_kernel, [((owned, pads), HALF), ((4 * cases + 8, BR), F32)], z, pad_rows, pad_cond)
    chunks = touched
    spots = 2 * (2 * REACH + 1)
    (places,) = call(places_kernel, [((touched * spots + 4, 8, BR), F32)], block_list)
    high, middle, low, top = call(
        split_kernel,
        [((inner, inner), HALF)] * 3 + [tile],
        matrix,
        far=range(1),
        scratch=[pltpu.VMEM((inner, inner), F32), semaphores((chunks,))],
        grant=49,
    )

    def collect(back, to_p1, to_p2):
        from_p2 = lax.ppermute(to_p2, "sub", far)
        to_p1 = to_p1 + lax.ppermute(back, "sub", swap)
        return to_p1, from_p2

    scale_there = lax.ppermute(precond, "sub", swap)
    four = barrier(jnp.stack([z, scale_there * lax.ppermute(rhs[0], "sub", swap)]))
    p2 = lax.ppermute(z, "sub", far)
    p1 = lax.ppermute(four, "sub", near)
    p1, p2, high, middle, low, top = barrier((p1, p2, high, middle, low, top))
    b = lax.ppermute(p1, "sub", swap)
    b, ones, pads_sent = barrier((b, ones, pads_sent))
    split = (places, high, middle, low)
    half = [((cases, inner), F32)] * 2
    back, to_p1, to_p2, kept, start_picked, start_product = call(
        first_kernel, [both, both, pair, both] + half, *split, p2, p1, four, b
    )
    late = call(late_kernel, [((LATE * BR, inner), HALF)] * 3, block_list, high, middle, low, scalar=(0,))
    conds = lax.ppermute(pads_sent, "board", across)
    local, start_jump, ones_there = call(
        ties_kernel,
        [full, ((cases, pads), F32), ((owned, pads), HALF)],
        z, pads_sent, conds, ones, sink,
    )
    to_p1, from_p2 = collect(back, to_p1, to_p2)
    from_p1 = lax.ppermute(to_p1, "sub", turned(near))
    from_p1, from_p2, late = barrier((from_p1, from_p2, late))
    (part,) = call(part_kernel, [((2 * blocks + 1, cases, BR), F32)], places, kept, local, from_p1, from_p2, precond, top)
    part_there = lax.ppermute(part, "sub", swap)
    part_across = lax.ppermute(part, "board", across)
    image, four, own, top = call(turn_kernel, [full, both, pair, tile], part, part_there, precond)
    known, guide, at_pads = call(
        shares_kernel,
        [((2, BR), F32), ((2, cases, BR), F32), ((cases, pads), F32)],
        rhs[0], z, image, own, ones, precond, sink, start_picked, start_product, start_jump, pads_sent, conds, top,
    )
    p1 = lax.ppermute(four, "sub", near)
    p2 = lax.ppermute(own, "sub", far)
    p1, p2, part_across, known, guide, at_pads = barrier((p1, p2, part_across, known, guide, at_pads))
    b = lax.ppermute(jnp.concatenate([p1, part_across[blocks : 2 * blocks]]), "sub", swap)
    early = call(second_early_kernel, half, *split, p2, p1, own, four[blocks:], top)
    b, early = barrier((b, early))
    tiles = cases // 8
    pair_tiles = ((2 * tiles, 8, BR), F32)
    sent = ((2 * tiles + 1, 8, BR), F32)
    given, stays, to_p2, sums = call(
        second_kernel,
        [((6 * tiles, 8, BR), F32)] * 2 + [sent, ((everyone, 4, BR), F32)],
        places, *late, own, b, *early, part_across, conds, pads_sent, ones, ones_there, at_pads, sink, top,
        start_picked, start_product, start_jump, z, known, guide,
    )
    given = lax.ppermute(given, "sub", swap)
    to_e, to_o, own_part = call(sort_kernel, [sent, sent, pair_tiles], places, given, stays, top)
    to_e, to_o, to_p2 = barrier((to_e, to_o, to_p2))
    from_o = lax.ppermute(to_o, "sub", beside(count))
    from_e = lax.ppermute(to_e, "sub", [(i, i ^ 2) for i in range(count)])
    from_p2 = lax.ppermute(to_p2, "sub", far)
    all_sums = lax.all_to_all(sums, ("board", "sub"), 0, 0)
    from_o, from_e, from_p2, all_sums = barrier((from_o, from_e, from_p2, all_sums))
    (steps,) = call(steps_kernel, [((3, cases, BR), F32)], all_sums)
    solution, residual = call(
        end_kernel,
        [full, full],
        rhs[0], z, image, own, places, own_part, from_e, from_o, from_p2, top, steps,
    )
    return (solution[None], residual[None])


def solution(mesh):
    in_specs = (
        P("board", None, "sub"),
        P("board", "sub", None),
        P("board", "sub"),
        P("board", "sub"),
        P("board", "sub"),
        P("board", "sub"),
        P("board", "sub"),
    )
    out_specs = (P("board", None, "sub"), P("board", None, "sub"))
    return jax.shard_map(
        on_device, mesh=mesh, in_specs=in_specs, out_specs=out_specs, check_vma=False
    )
```

```python
import jax
import jax.numpy as jnp
from jax import lax
from jax.experimental import pallas as pl
from jax.experimental.pallas import tpu as pltpu
from jax.sharding import PartitionSpec as P

BR = 128
REACH = 3
F32 = jnp.float32
HALF = jnp.bfloat16
barrier = lax.optimization_barrier


def climb(count, step):
    pairs = []
    for source in range(count):
        chip, core = divmod(source, 2)
        target = chip - step if core else chip + step
        inside = 0 <= target < count // 2
        pairs.append((source, target * 2 + core if inside else source ^ 1))
    return pairs


def leap(count):
    pairs = []
    for source in range(count):
        chip, core = divmod(source, 2)
        target = chip + 2 if core else chip - 2
        if 0 <= target < count // 2:
            pairs.append((source, target * 2 + 1 - core))
        else:
            pairs.append((source, source ^ 2))
    return pairs


def beside(count):
    pairs = []
    for source in range(count):
        chip, core = divmod(source, 2)
        target = chip + 1 if chip % 2 else chip - 1
        inside = 0 <= target < count // 2
        pairs.append((source, target * 2 + core if inside else source ^ 1))
    return pairs


def turned(pairs):
    return [(target, source) for source, target in pairs]


def thirds(value):
    high = value.astype(HALF)
    rest = value - high.astype(F32)
    middle = rest.astype(HALF)
    return high, middle, (rest - middle.astype(F32)).astype(HALF)


def dot(left, right):
    return jnp.dot(left, right, preferred_element_type=F32)


def times_ones(value, ones, turn):
    rows = value.shape[0]
    parts = jnp.concatenate(thirds(value))
    if turn:
        out = lax.dot_general(parts, ones, (((1,), (1,)), ((), ())), preferred_element_type=F32)
    else:
        out = dot(parts, ones)
    return out[:rows] + (out[rows : 2 * rows] + out[2 * rows :])


def pad_matrix(pad_rows, owned):
    here = lax.broadcasted_iota(jnp.int32, (owned, pad_rows.shape[1]), 0)
    return (here == pad_rows).astype(F32).astype(HALF)


def product_of(value, high, middle, low):
    rows = value.shape[0]
    one, two, three = thirds(value)
    first = dot(jnp.concatenate([one, two, three]), high[...])
    second = dot(jnp.concatenate([one, two]), middle[...])
    small = first[2 * rows :] + second[rows:] + dot(one, low[...])
    return (small + (first[rows : 2 * rows] + second[:rows])) + first[:rows]


def wide(pair):
    return jnp.concatenate([pair[0], pair[1]], axis=1)


def put_wide(ref, start, value):
    ref[start] = value[:, :BR]
    ref[start + 1] = value[:, BR:]


def lanes_of(cases, slot):
    lane = lax.broadcasted_iota(jnp.int32, (cases, BR), 1)
    return lane == lax.broadcasted_iota(jnp.int32, (cases, BR), 0) + slot * cases


def as_column(row, slot, cases):
    return jnp.sum(jnp.where(lanes_of(cases, slot), row, 0.0), axis=1, keepdims=True)


def begin_kernel(z, pad_rows, pad_cond, ones_out, pads_out):
    cases = z.shape[0]
    owned, count = ones_out.shape
    ones = pad_matrix(pad_rows[...], owned)
    ones_out[...] = ones
    pads_out[...] = jnp.zeros_like(pads_out)
    pads_out[:cases, :count] = times_ones(z[...], ones, False)
    pads_out[cases : cases + 1, :count] = pad_cond[...]
    pads_out[cases + 8 : cases + 9, :count] = pad_rows[...].astype(F32)


def places_kernel(blocks, places):
    position = lax.axis_index("sub")
    chip, core = position // 2, lax.rem(position, 2)
    above, below = lax.axis_size("sub") // 2 - 1 - chip, chip
    touched = blocks.shape[1]
    listed = blocks[...]
    offset = listed // 2 - position
    mirrored = jnp.where(core == 0, offset, -offset)
    place = jnp.where(mirrored == 2, 6, jnp.where(mirrored == 3, 5, mirrored + REACH))
    place = place * 2 + lax.rem(listed, 2)
    spots = 2 * (2 * REACH + 1)
    for i in range(touched):
        here = jnp.broadcast_to(place[:, i : i + 1], places.shape[1:])
        for j in range(spots):
            places[i * spots + j] = (here == j).astype(F32)
    near = jnp.where(core == 0, above, below) >= 1
    far = jnp.where(core == 0, below, above) >= 2
    odd = lax.rem(chip, 2) == 1
    cross = jnp.where(odd, above, below) >= 1
    inner = odd == (core == 0)
    for i, sender in enumerate((near, far, cross, inner)):
        places[touched * spots + i] = jnp.full(places.shape[1:], sender.astype(F32))


def split_kernel(schur, high, middle, low, top, held, sems):
    chunk = held.shape[0] // sems.shape[0]
    copies = []
    for i in range(sems.shape[0]):
        rows = slice(i * chunk, (i + 1) * chunk)
        copies.append(pltpu.make_async_copy(schur.at[rows], held.at[rows], sems.at[i]))
    for copy in copies:
        copy.start()
    largest = jnp.ones((1, chunk), F32)
    for i, copy in enumerate(copies):
        rows = slice(i * chunk, (i + 1) * chunk)
        copy.wait()
        high[rows], middle[rows], low[rows] = thirds(0.25 * held[rows])
        largest = jnp.maximum(largest, jnp.max(held[rows, rows], axis=0, keepdims=True))
    top[...] = jnp.broadcast_to(jnp.max(largest, axis=1, keepdims=True), top.shape)


def late_kernel(blocks, high, middle, low, late_high, late_middle, late_low):
    position = lax.axis_index("sub")
    core = lax.rem(position, 2)
    touched = blocks.shape[1]
    spots = []
    for i in range(touched):
        offset = blocks[0, i] // 2 - position
        mirrored = jnp.where(core == 0, offset, -offset)
        place = jnp.where(mirrored == 2, 6, jnp.where(mirrored == 3, 5, mirrored + REACH))
        spots.append(place * 2 + lax.rem(blocks[0, i], 2))
    for j in range(LATE):
        source = jnp.int32(-1)
        for i in range(touched):
            source = jnp.where(spots[i] == SPOTS - LATE + j, i, source)
        rows = pl.ds(pl.multiple_of(jnp.maximum(source, 0) * BR, BR), BR)
        keep = jnp.where(source >= 0, 1.0, 0.0)
        for part, late in ((high, late_high), (middle, late_middle), (low, late_low)):
            late[j * BR : (j + 1) * BR] = (part[rows].astype(F32) * keep).astype(HALF)


def spot(places, i, cases):
    return jnp.concatenate([places[i]] * (cases // 8))


SPOTS = 2 * (2 * REACH + 1)
LATE = 4


def picked_blocks(places, held, touched, begin):
    cases = held[0].shape[0]
    picked = []
    for i in range(touched):
        total = spot(places, i * SPOTS + begin, cases) * held[0]
        for j in range(1, len(held)):
            total = total + spot(places, i * SPOTS + begin + j, cases) * held[j]
        picked.append(total)
    return jnp.concatenate(picked, axis=1)


def landed_blocks(places, product):
    cases, touched = product.shape[0], product.shape[1] // BR
    spots = (places.shape[0] - 4) // touched
    landed = []
    for j in range(spots):
        total = spot(places, j, cases) * product[:, :BR]
        for i in range(1, touched):
            total = total + spot(places, i * spots + j, cases) * product[:, i * BR : (i + 1) * BR]
        landed.append(total)
    return landed


def halves(*values):
    return [value[:, start : start + BR] for value in values for start in (0, BR)]


def mean_of(mine, conds, cases, count):
    return 0.5 * (mine[cases : cases + 1, :count] + conds[cases : cases + 1, :count])


def first_kernel(
    places, high, middle, low, p2, p1, four, b, back, to_p1, to_p2, kept, picked_out, product_out
):
    picked = picked_blocks(places, halves(p2, p1[0], p1[1], four[0], four[1], b[0], b[1]), high.shape[0] // BR, 0)
    product = product_of(4.0 * picked, high, middle, low)
    landed = landed_blocks(places, product)
    for j in range(2):
        to_p2[j] = landed[j]
    for j in range(4):
        back[j] = landed[10 + j]
        to_p1[j] = landed[2 + j]
    for j in range(4):
        kept[j] = landed[6 + j]
    picked_out[...] = picked
    product_out[...] = product


def ties_kernel(z, mine, conds, ones, sink, local, jump_out, ones_there):
    cases, count = z.shape[0], ones.shape[1]
    jump = mine[:cases, :count] - conds[:cases, :count]
    jump_out[...] = jump
    pads = conds[cases + 8 : cases + 9, :count].astype(jnp.int32)
    ones_there[...] = pad_matrix(pads, z.shape[1])
    local[...] = sink[...] * z[...] + times_ones(mean_of(mine, conds, cases, count) * jump, ones[...], True)


def folded(value):
    total = value[:, :BR]
    for i in range(1, value.shape[1] // BR):
        total = total + value[:, i * BR : (i + 1) * BR]
    return total


def across_lanes(value):
    return jnp.sum(value, axis=1, keepdims=True)


def largest_of(blocks, pads):
    size = jnp.maximum(
        jnp.max(jnp.abs(blocks), axis=1, keepdims=True), jnp.max(jnp.abs(pads), axis=1, keepdims=True)
    )
    return jnp.where(size > 0.0, size, 1.0)


def case_row(columns):
    cases = columns[0].shape[0]
    total = jnp.where(lanes_of(cases, 0), columns[0], 0.0)
    for slot in range(1, len(columns)):
        total = jnp.where(lanes_of(cases, slot), columns[slot], total)
    return jnp.sum(total, axis=0, keepdims=True)


def shares_kernel(
    rhs, z, image, scaled, ones, precond, sink, picked, product, jump, mine, conds, top, known, guide, at_pads
):
    cases, count = jump.shape
    at_pads[...] = times_ones(wide(scaled), ones[...], False)
    start = z[...]
    bulk = 0.25 * (4.0 / top[0:1, 0:1])
    mean = mean_of(mine, conds, cases, count)
    size = largest_of(picked[...], jump[...])
    inverse = 1.0 / size
    unit = picked[...] * inverse
    unit_jump = jump[...] * inverse
    unit_own = start * inverse
    pulled = (product[...] * bulk) * inverse
    energy = across_lanes(folded(unit * pulled) + bulk * folded(sink[...] * unit_own * unit_own))
    energy = energy + 0.5 * bulk * across_lanes(mean * unit_jump * unit_jump)
    norm = across_lanes(folded(rhs[...] * start))
    curve = across_lanes(folded(start * image[...]))
    reach = jnp.max(jnp.abs(image[...]), axis=1, keepdims=True)
    still = reach <= 0.0
    scale = jnp.clip(size / jnp.where(still, 1.0, reach), 1e-34, 1e30)
    guess = jnp.where(curve > 0.0, norm / jnp.where(curve > 0.0, curve, 1.0), 0.0)
    guess = jnp.where(still, 1.0, jnp.clip(guess, scale * (1.0 / 1024.0), scale * 8.0))
    moved = guess * image[...]
    rest = rhs[...] - moved
    weighted = precond[...] * moved
    known[0:1] = case_row([norm, guess, across_lanes(folded(precond[...] * rest * rest)), across_lanes(folded(weighted * rest))])
    known[1:2] = case_row(
        [across_lanes(folded(weighted * moved)), size, energy, jnp.broadcast_to(top[0:1, 0:1], size.shape)]
    )
    tilt = jnp.where(norm > 0.0, curve / jnp.where(norm > 0.0, norm, 1.0), 0.0) * size
    guide[0] = jnp.broadcast_to(jnp.clip(tilt, -1e37, 1e37), guide.shape[1:])
    guide[1] = jnp.broadcast_to(inverse, guide.shape[1:])


def put_tiles(ref, start, block):
    tiles = block.shape[0] // 8
    ref[start * tiles : (start + 1) * tiles] = block.reshape(tiles, 8, BR)


def second_early_kernel(places, high, middle, low, p2, p1, own, a, top, picked_out, product_out):
    held = [p2[0], p2[1], p1[0], p1[1], p1[2], p1[3], own[0], own[1], a[0], a[1]]
    picked = picked_blocks(places, held, high.shape[0] // BR, 0)
    picked_out[...] = picked
    product_out[...] = product_of((picked * (4.0 / top[0:1, 0:1])) * (1.0 / 1024.0), high, middle, low)


def second_kernel(
    places, high, middle, low, own, b, early, early_product, there, conds, mine, ones, ones_there, at_pads, sink, top,
    start_picked, start_product, start_jump, start_own, known, guide,
    given, stays, to_p2, sums,
):
    cases = own.shape[1]
    count = ones.shape[1]
    less = 4.0 / top[0:1, 0:1]
    held = [b[j] for j in range(LATE)]
    picked = early[...] + picked_blocks(places, held, early.shape[1] // BR, SPOTS - LATE)
    late = (jnp.concatenate(held, axis=1) * less) * (1.0 / 1024.0)
    product = early_product[...] + product_of(late, high, middle, low)
    scales = jnp.concatenate([there[4, 0:1], there[4, 1:2]], axis=1)
    values = scales * wide(there[0:2] + b[4:6])
    here = wide(own)
    jump = at_pads[...] - times_ones(values, ones_there[...], False)
    mean = mean_of(mine, conds, cases, count)
    local = sink[...] * here + times_ones(mean * jump, ones[...], True)
    local = (local * less) * (1.0 / 4096.0)
    size = largest_of(picked, jump)
    inverse = 1.0 / size
    bulk = 0.25 * less
    tilt = jnp.clip(guide[0, :, 0:1] * inverse, -1e3, 1e3)
    unit = guide[1, :, 0:1]
    tilted = tilt * unit
    rest = picked * inverse - tilted * start_picked[...]
    pulled = product * (1024.0 * inverse) - (start_product[...] * bulk) * tilted
    rest_own = here * inverse - tilted * start_own[...]
    rest_jump = jump * inverse - tilted * start_jump[...]
    sunk = sink[...] * rest_own
    tied = 0.5 * mean * rest_jump
    tail = jnp.zeros((cases, BR - count), F32)
    energy = folded(rest * pulled) + bulk * folded(sunk * rest_own)
    energy = energy + bulk * jnp.concatenate([tied * rest_jump, tail], axis=1)
    cross = folded(start_picked[...] * unit * pulled) + bulk * folded(sunk * (start_own[...] * unit))
    cross = cross + bulk * jnp.concatenate([tied * (start_jump[...] * unit), tail], axis=1)
    own_row = case_row([size, tilt, across_lanes(cross), across_lanes(energy)])
    total = jnp.concatenate([known[0:2], own_row, jnp.zeros_like(own_row)])
    sums[...] = jnp.broadcast_to(total[None], sums.shape)
    landed = landed_blocks(places, product)
    for j in range(2):
        put_tiles(to_p2, j, landed[j])
        put_tiles(given, j, landed[4 + j])
        put_tiles(given, 2 + j, landed[10 + j])
        put_tiles(given, 4 + j, landed[8 + j])
        put_tiles(stays, j, landed[2 + j])
        put_tiles(stays, 2 + j, landed[12 + j])
        put_tiles(stays, 4 + j, landed[6 + j] + local[:, j * BR : (j + 1) * BR])
    to_p2[to_p2.shape[0] - 1] = top[...]


def part_kernel(places, kept, local, from_p1, from_p2, precond, top, part):
    cases = kept.shape[1]
    near, far = [spot(places, places.shape[0] - 4 + i, cases)[None] for i in range(2)]
    one = from_p1[...] * near
    mine = kept[0:2] + one[0:2] + from_p2[...] * far
    part[0] = mine[0] + local[:, :BR]
    part[1] = mine[1] + local[:, BR:]
    part[2:4] = kept[2:4] + one[2:4]
    part[4] = jnp.zeros(part.shape[1:], F32)
    part[4, 0:1] = precond[:, :BR]
    part[4, 1:2] = precond[:, BR:]
    part[4, 8:16] = top[...]


def turn_kernel(part, there, precond, image_out, both_out, own_out, top_out):
    image = wide(part[0:2] + there[2:4])
    other = part[2:4] + there[0:2]
    image_out[...] = image
    scaled = precond[...] * image
    put_wide(both_out, 0, scaled)
    put_wide(own_out, 0, scaled)
    both_out[2] = there[4, 0:1] * other[0]
    both_out[3] = there[4, 1:2] * other[1]
    top_out[...] = jnp.maximum(part[4, 8:16], there[4, 8:16])


def sort_kernel(places, given, stays, top, to_e, to_o, own):
    pair = stays.shape[0] // 3
    inner = places[places.shape[0] - 1] > 0.0
    for i in range(pair):
        near = stays[i] + given[pair + i]
        away = stays[pair + i] + given[i]
        to_e[i] = jnp.where(inner, near, away)
        to_o[i] = jnp.where(inner, away, near)
        own[i] = stays[2 * pair + i] + given[2 * pair + i]
    to_e[pair] = top[...]
    to_o[pair] = top[...]


def steps_of(sums, cases):
    rows = [sums[:, i, :] for i in range(3)]

    def value(i):
        row = rows[i // 4]
        return row if i % 4 == 0 else pltpu.roll(row, BR - (i % 4) * cases, 1)

    norm, guess, rest, mixed, moved, size, energy, top, other_size, tilt, cross, other_energy = [
        value(i) for i in range(12)
    ]

    def everyone(terms):
        return jnp.sum(terms, axis=0, keepdims=True)

    norm = everyone(norm)
    alpha = norm / everyone((size * size * energy) * top)
    shift = alpha / guess - 1.0
    fresh = everyone(rest + shift * (shift * moved - 2.0 * mixed))
    grown = 1.0 + fresh / norm
    two = alpha * other_size
    one = grown * size - two * tilt
    bend = everyone(((one * one) * energy + two * (two * other_energy - 2.0 * one * cross)) * top)
    return [as_column(row, 0, cases) for row in (alpha, grown, fresh / bend)]


def end_kernel(rhs, z, image, scaled, places, own, from_e, from_o, from_p2, top, sums, solution, residual):
    cases = solution.shape[0]
    tiles = cases // 8
    alpha, grown, step = steps_of(sums, cases)
    start = z[...]
    direction = grown * start - alpha * wide(scaled)
    solution[...] = alpha * start + step * direction
    one = jnp.ones_like(top)
    cross, far = places[places.shape[0] - 2], places[places.shape[0] - 3]
    parts = [(own, top[...], one)] + [
        (part, part[2 * tiles], valid) for part, valid in ((from_e, one), (from_o, cross), (from_p2, far))
    ]
    most = top[...]
    for _, scale, valid in parts[1:]:
        most = jnp.maximum(most, valid * scale)
    total = 0.0
    for part, scale, valid in parts:
        factor = valid * (scale / most)
        total = total + part[: 2 * tiles] * factor[None]
    blocks = total.reshape(2, cases, BR)
    bulk = spot([most], 0, cases)
    second = ((alpha * wide(blocks)) * wide([bulk, bulk])) * 1024.0
    residual[...] = rhs[...] - alpha * image[...] - step * (grown * image[...] - second)


def call(kernel, outs, *operands, scratch=(), far=(), scalar=(), grant=32):
    def space(outside, i):
        return pl.BlockSpec(memory_space=pl.ANY if i in outside else pltpu.VMEM)

    return pl.pallas_call(
        kernel,
        in_specs=[pl.BlockSpec(memory_space=pltpu.SMEM) if i in scalar else space(far, i) for i in range(len(operands))],
        out_specs=[space((), i) for i in range(len(outs))],
        out_shape=[jax.ShapeDtypeStruct(shape, kind) for shape, kind in outs],
        scratch_shapes=list(scratch),
        compiler_params=pltpu.CompilerParams(vmem_limit_bytes=grant * 1024 * 1024),
    )(*operands)


def on_device(rhs, schur, block_list, pad_rows, pad_cond, sink, precond):
    matrix = schur[0]
    cases, owned = rhs.shape[1:]
    inner = matrix.shape[0]
    blocks = owned // BR
    touched = inner // BR
    count = lax.axis_size("sub")
    everyone = count * lax.axis_size("board")
    pads = pad_rows.shape[1]
    swap = [(i, i ^ 1) for i in range(count)]
    across = [(i, i ^ 1) for i in range(lax.axis_size("board"))]
    near, far = climb(count, 1), leap(count)
    pair = ((blocks, cases, BR), F32)
    both = ((2 * blocks, cases, BR), F32)
    tile = ((8, BR), F32)
    full = ((cases, owned), F32)
    semaphores = pltpu.SemaphoreType.DMA

    z = barrier(precond * rhs[0])
    ones, pads_sent = call(begin_kernel, [((owned, pads), HALF), ((4 * cases + 8, BR), F32)], z, pad_rows, pad_cond)
    chunks = touched
    spots = 2 * (2 * REACH + 1)
    (places,) = call(places_kernel, [((touched * spots + 4, 8, BR), F32)], block_list)
    high, middle, low, top = call(
        split_kernel,
        [((inner, inner), HALF)] * 3 + [tile],
        matrix,
        far=range(1),
        scratch=[pltpu.VMEM((inner, inner), F32), semaphores((chunks,))],
        grant=49,
    )

    def collect(back, to_p1, to_p2):
        from_p2 = lax.ppermute(to_p2, "sub", far)
        to_p1 = to_p1 + lax.ppermute(back, "sub", swap)
        return to_p1, from_p2

    scale_there = lax.ppermute(precond, "sub", swap)
    four = barrier(jnp.stack([z, scale_there * lax.ppermute(rhs[0], "sub", swap)]))
    p2 = lax.ppermute(z, "sub", far)
    p1 = lax.ppermute(four, "sub", near)
    p1, p2, high, middle, low, top = barrier((p1, p2, high, middle, low, top))
    b = lax.ppermute(p1, "sub", swap)
    b, ones, pads_sent = barrier((b, ones, pads_sent))
    split = (places, high, middle, low)
    half = [((cases, inner), F32)] * 2
    back, to_p1, to_p2, kept, start_picked, start_product = call(
        first_kernel, [both, both, pair, both] + half, *split, p2, p1, four, b
    )
    late = call(late_kernel, [((LATE * BR, inner), HALF)] * 3, block_list, high, middle, low, scalar=(0,))
    conds = lax.ppermute(pads_sent, "board", across)
    local, start_jump, ones_there = call(
        ties_kernel,
        [full, ((cases, pads), F32), ((owned, pads), HALF)],
        z, pads_sent, conds, ones, sink,
    )
    to_p1, from_p2 = collect(back, to_p1, to_p2)
    from_p1 = lax.ppermute(to_p1, "sub", turned(near))
    from_p1, from_p2, late = barrier((from_p1, from_p2, late))
    (part,) = call(part_kernel, [((2 * blocks + 1, cases, BR), F32)], places, kept, local, from_p1, from_p2, precond, top)
    part_there = lax.ppermute(part, "sub", swap)
    part_across = lax.ppermute(part, "board", across)
    image, four, own, top = call(turn_kernel, [full, both, pair, tile], part, part_there, precond)
    known, guide, at_pads = call(
        shares_kernel,
        [((2, BR), F32), ((2, cases, BR), F32), ((cases, pads), F32)],
        rhs[0], z, image, own, ones, precond, sink, start_picked, start_product, start_jump, pads_sent, conds, top,
    )
    p1 = lax.ppermute(four, "sub", near)
    p2 = lax.ppermute(own, "sub", far)
    p1, p2, part_across, known, guide, at_pads = barrier((p1, p2, part_across, known, guide, at_pads))
    b = lax.ppermute(jnp.concatenate([p1, part_across[blocks : 2 * blocks]]), "sub", swap)
    early = call(second_early_kernel, half, *split, p2, p1, own, four[blocks:], top)
    b, early = barrier((b, early))
    tiles = cases // 8
    pair_tiles = ((2 * tiles, 8, BR), F32)
    sent = ((2 * tiles + 1, 8, BR), F32)
    given, stays, to_p2, sums = call(
        second_kernel,
        [((6 * tiles, 8, BR), F32)] * 2 + [sent, ((everyone, 4, BR), F32)],
        places, *late, own, b, *early, part_across, conds, pads_sent, ones, ones_there, at_pads, sink, top,
        start_picked, start_product, start_jump, z, known, guide,
    )
    given = lax.ppermute(given, "sub", swap)
    to_e, to_o, own_part = call(sort_kernel, [sent, sent, pair_tiles], places, given, stays, top)
    to_e, to_o, to_p2 = barrier((to_e, to_o, to_p2))
    from_o = lax.ppermute(to_o, "sub", beside(count))
    from_e = lax.ppermute(to_e, "sub", [(i, i ^ 2) for i in range(count)])
    from_p2 = lax.ppermute(to_p2, "sub", far)
    all_sums = lax.all_to_all(sums, ("board", "sub"), 0, 0)
    from_o, from_e, from_p2, all_sums = barrier((from_o, from_e, from_p2, all_sums))
    solution, residual = call(
        end_kernel,
        [full, full],
        rhs[0], z, image, own, places, own_part, from_e, from_o, from_p2, top, all_sums,
    )
    return (solution[None], residual[None])


def solution(mesh):
    in_specs = (
        P("board", None, "sub"),
        P("board", "sub", None),
        P("board", "sub"),
        P("board", "sub"),
        P("board", "sub"),
        P("board", "sub"),
        P("board", "sub"),
    )
    out_specs = (P("board", None, "sub"), P("board", None, "sub"))
    return jax.shard_map(
        on_device, mesh=mesh, in_specs=in_specs, out_specs=out_specs, check_vma=False
    )
```
